32 devices in a mesh: batch: 4 (over y, core), seq: 8 (over z, x).
Axes of the slice: x: 2, y: 2, z: 4, core: 2. Of those that a mesh axis runs over, the one named last changes fastest.
Arguments:
- inputs: bfloat16 [4, 1024, 2048], P('batch', 'seq'), may hold values from -6 to 6
- positions: int32 [4, 1024], P('batch', 'seq'), may hold values from 0 to 3069, as said below
- attn_gain: bfloat16 [2048], P(('batch', 'seq')), may hold values from 0.5 to 1.5
- q_weight: bfloat16 [2048, 2048], P(('batch', 'seq')), may hold values from -0.125 to 0.125
- k_weight: bfloat16 [2048, 512], P(('batch', 'seq')), may hold values from -0.125 to 0.125
- v_weight: bfloat16 [2048, 512], P(('batch', 'seq')), may hold values from -0.125 to 0.125
- o_weight: bfloat16 [2048, 2048], P(('batch', 'seq')), may hold values from -0.5 to 0.5
- ffn_gain: bfloat16 [2048], P(('batch', 'seq')), may hold values from 0.5 to 1.5
- gate_weight: bfloat16 [2048, 8192], P(('batch', 'seq')), may hold values from -0.125 to 0.125
- up_weight: bfloat16 [2048, 8192], P(('batch', 'seq')), may hold values from -0.125 to 0.125
- down_weight: bfloat16 [2048, 8192], P(('batch', 'seq')), may hold values from -0.0625 to 0.0625
- cotangent: bfloat16 [4, 1024, 2048], P('batch', 'seq'), may hold values from -6 to 6
Outputs:
- output: bfloat16 [4, 1024, 2048], P('batch', 'seq')
- input_grad: float32 [4, 1024, 2048], P('batch', 'seq')
- attn_gain_grad: float32 [2048], P(('batch', 'seq'))
- q_grad: float32 [2048, 2048], P(('batch', 'seq'))
- k_grad: float32 [2048, 512], P(('batch', 'seq'))
- v_grad: float32 [2048, 512], P(('batch', 'seq'))
- o_grad: float32 [2048, 2048], P(('batch', 'seq'))
- ffn_gain_grad: float32 [2048], P(('batch', 'seq'))
- gate_grad: float32 [2048, 8192], P(('batch', 'seq'))
- up_grad: float32 [2048, 8192], P(('batch', 'seq'))
- down_grad: float32 [2048, 8192], P(('batch', 'seq'))
The draws below stay inside these ranges and needn't reach their ends.
Inputs may be any that keep to these rules, and one draw needn't show every extreme that they name: Within a sequence the positions rise by one or two from token to token, from a start between 0 and 1023.
All inputs are finite; a program needn't handle non-finite values.
Results may differ from the reference program's by a relative error of at most 0.015.
Values may be sent and summed in bfloat16 or wider, within the bound.
No kernel may reach another device: no remote copies, remote signals or barrier semaphores. Data moves between devices by JAX's collectives and lax.ppermute only.
A program may use at most 768 MiB of HBM per device.

```python
import math
import jax
import jax.numpy as jnp
from jax import lax

D = 2048
HEADS = 32
KV_HEADS = 8
HEAD_DIM = 64
FF = 8192
SEQS = 4
L = 1024
KV_EXP = 8


def draw_positions(key, part):
    key = jax.random.fold_in(key, 7)
    start_key = jax.random.fold_in(key, 1)
    step_key = jax.random.fold_in(key, 2)
    starts = jax.random.randint(start_key, (SEQS, 1), 0, L)
    starts = starts.at[0, 0].set(0).at[SEQS - 1, 0].set(L - 1)
    strides = jax.random.randint(step_key, (SEQS, L - 1), 1, 3)
    strides = strides.at[SEQS - 1, :].set(2)
    offsets = jnp.concatenate([jnp.zeros((SEQS, 1), jnp.int32), jnp.cumsum(strides, axis=1).astype(jnp.int32)], axis=1)
    return (starts + offsets).astype(jnp.int32)


def block_scale(key, shape, shards, smallest, top_value):
    level, own = 1.0, jax.random.fold_in(key, 6)
    for dim, parts in shards:
        draws = jnp.exp(jax.random.uniform(jax.random.fold_in(own, dim), (parts,), jnp.float32, smallest / len(shards), top_value / len(shards)))
        level = level * jnp.repeat(draws, shape[dim] // parts).reshape([-1 if axis == dim else 1 for axis in range(len(shape))])
    return level


def scatter_about(own_key, dims, width, most, shards=(), held_as=jnp.bfloat16):
    loudness = block_scale(own_key, dims, shards, -0.22, 0.18) if shards else 1.0
    drawn = jax.random.normal(own_key, dims, jnp.float32) * width * loudness
    return jnp.minimum(jnp.maximum(drawn, -most), most).astype(held_as)


def setup_inputs(seed: int = 0) -> dict:
    key_of = jax.random.split(jax.random.key(seed), 13)
    inputs = scatter_about(key_of[0], (SEQS, L, D), 1.0, 6.0, ((0, 4), (1, 8)))
    positions = draw_positions(jax.random.fold_in(key_of[12], 71), 0)
    attn_gain = jnp.clip(1.0 + 0.1 * jax.random.normal(key_of[2], (D,), jnp.float32), 0.5, 1.5).astype(jnp.bfloat16)
    q_weight = scatter_about(key_of[3], (D, HEADS * HEAD_DIM), D ** -0.5, 0.125, ((0, 32),))
    k_weight = scatter_about(key_of[4], (D, KV_HEADS * HEAD_DIM), D ** -0.5, 0.125, ((0, 32),))
    v_weight = scatter_about(key_of[5], (D, KV_HEADS * HEAD_DIM), D ** -0.5, 0.125, ((0, 32),))
    o_weight = scatter_about(key_of[6], (D, HEADS * HEAD_DIM), (HEADS * HEAD_DIM // 16) ** -0.5, 0.5, ((0, 32),))
    ffn_gain = jnp.clip(1.0 + 0.1 * jax.random.normal(key_of[7], (D,), jnp.float32), 0.5, 1.5).astype(jnp.bfloat16)
    gate_weight = scatter_about(key_of[8], (D, FF), D ** -0.5, 0.125, ((0, 32),))
    up_weight = scatter_about(key_of[9], (D, FF), D ** -0.5, 0.125, ((0, 32),))
    down_weight = scatter_about(key_of[10], (D, FF), FF ** -0.5, 0.0625, ((0, 32),))
    cotangent = scatter_about(key_of[11], (SEQS, L, D), 1.0, 6.0, ((0, 4), (1, 8)))
    return {"inputs": inputs, "positions": positions, "attn_gain": attn_gain, "q_weight": q_weight, "k_weight": k_weight, "v_weight": v_weight, "o_weight": o_weight, "ffn_gain": ffn_gain, "gate_weight": gate_weight, "up_weight": up_weight, "down_weight": down_weight, "cotangent": cotangent}


@jax.custom_vjp
def low(v):
    return lax.optimization_barrier(v.astype(jnp.bfloat16)).astype(jnp.float32)

@jax.custom_vjp
def low_back(v):
    return v

def low_keep(v):
    return (low(v), None)

def low_pass(kept, grad):
    return (grad,)

def back_keep(v):
    return (v, None)

def back_low(kept, grad):
    return (low(grad),)
low.defvjp(low_keep, low_pass)
low_back.defvjp(back_keep, back_low)
epsilon = 1e-05
rope_base = 500000.0
rope_scale = 32.0
low_freq = 1.0
high_freq = 4.0
initial_context = 8192.0

def matmul(left, right):
    return jnp.dot(left, right, precision=lax.Precision.HIGHEST)

def rms_norm(values, gain):
    factor = lax.rsqrt(lax.optimization_barrier(jnp.mean(values * values, axis=-1, keepdims=True)) + epsilon)
    return values * factor * gain

def frequencies():
    half = HEAD_DIM // 2
    base_freqs = rope_base ** (-(jnp.arange(half, dtype=jnp.float32) * 2.0 / HEAD_DIM))
    wavelen = 2.0 * math.pi / base_freqs
    smooth = (initial_context / wavelen - low_freq) / (high_freq - low_freq)
    middle = (1.0 - smooth) * base_freqs / rope_scale + smooth * base_freqs
    return jnp.where(wavelen < initial_context / high_freq, base_freqs, jnp.where(wavelen > initial_context / low_freq, base_freqs / rope_scale, middle))

def angles_of(positions):
    freqs = frequencies()
    turned = positions.astype(jnp.float32)[:, None] * freqs[None, :]
    return (jnp.cos(turned)[:, None, :], jnp.sin(turned)[:, None, :])

def rotate(values, cosine, sine):
    half = values.shape[-1] // 2
    first_half = values[..., :half]
    second_half = values[..., half:]
    return jnp.concatenate([first_half * cosine - second_half * sine, second_half * cosine + first_half * sine], axis=-1)

def attention(grouped, keys_exp, values_exp):
    block_rows = min(512, L)
    blocks = L // block_rows

    def one_block(block_index):
        offset = block_index * block_rows
        query_block = lax.dynamic_slice_in_dim(grouped, offset, block_rows, 0)
        scores = jnp.einsum('qegd,ked->egqk', query_block, keys_exp, precision=lax.Precision.HIGHEST) * HEAD_DIM ** (-0.5)
        scores = low_back(scores)
        row_ids = offset + jnp.arange(block_rows, dtype=jnp.int32)
        col_ids = jnp.arange(L, dtype=jnp.int32)
        scores = jnp.where(col_ids[None, :] <= row_ids[:, None], scores, -1e+30)
        peak = lax.optimization_barrier(jnp.max(scores, axis=-1, keepdims=True))
        expd = jnp.exp(scores - peak)
        probs = low(expd / lax.optimization_barrier(jnp.sum(expd, axis=-1, keepdims=True)))
        return jnp.einsum('egqk,ked->qegd', probs, values_exp, precision=lax.Precision.HIGHEST)
    result = lax.map(jax.checkpoint(one_block), jnp.arange(blocks, dtype=jnp.int32))
    return result.reshape(L, KV_EXP, HEADS // KV_EXP, HEAD_DIM)

def sequence_forward(weights, pair):
    token_states, positions = pair
    attn_gain, q_weight, k_weight, v_weight, o_weight, ffn_gain, gate_weight, up_weight, down_weight = weights
    cosine, sine = angles_of(positions)
    copies = KV_EXP // KV_HEADS
    normed = low(rms_norm(token_states, attn_gain))
    queries = low_back(matmul(normed, q_weight)).reshape(L, HEADS, HEAD_DIM)
    keys = low_back(matmul(normed, k_weight)).reshape(L, KV_HEADS, HEAD_DIM)
    values = low_back(matmul(normed, v_weight)).reshape(L, KV_HEADS, HEAD_DIM)
    queries_rot = low(low_back(rotate(queries, cosine, sine)))
    keys_rot = low(rotate(keys, cosine, sine))
    keys_exp = low_back(jnp.repeat(keys_rot, copies, axis=1))
    values_exp = low_back(jnp.repeat(low(values), copies, axis=1))
    grouped = queries_rot.reshape(L, KV_EXP, HEADS // KV_EXP, HEAD_DIM)
    attended = attention(grouped, keys_exp, values_exp)
    attn_out = low(low_back(attended.reshape(L, HEADS * HEAD_DIM)))
    hidden1 = token_states + low_back(matmul(attn_out, o_weight.T))
    normed2 = low(rms_norm(hidden1, ffn_gain))
    gate = low_back(matmul(normed2, gate_weight))
    upper = low_back(matmul(normed2, up_weight))
    hidden = low(jax.nn.silu(gate) * upper)
    return hidden1 + low_back(matmul(hidden, down_weight.T))

def reference(inputs, positions, attn_gain, q_weight, k_weight, v_weight, o_weight, ffn_gain, gate_weight, up_weight, down_weight, cotangent):
    weights = tuple((item.astype(jnp.float32) for item in (attn_gain, q_weight, k_weight, v_weight, o_weight, ffn_gain, gate_weight, up_weight, down_weight)))
    token_states = inputs.astype(jnp.float32)

    def forward(token_states, weights):
        return lax.map(lambda pair: sequence_forward(weights, pair), (token_states, positions))
    result, pullback = jax.vjp(forward, token_states, weights)
    token_grad, weight_grads = pullback(cotangent.astype(jnp.float32))
    attn_gain_grad, q_grad, k_grad, v_grad, o_grad, ffn_gain_grad, gate_grad, up_grad, down_grad = weight_grads
    return (result.astype(jnp.bfloat16), token_grad, attn_gain_grad, q_grad, k_grad, v_grad, o_grad, ffn_gain_grad, gate_grad, up_grad, down_grad)
```

```python
import math

import jax
import jax.numpy as jnp
from jax import lax
from jax.sharding import PartitionSpec as P

HEADS = 32
KV_HEADS = 8
HEAD_DIM = 64

epsilon = 1e-05
rope_base = 500000.0
rope_scale = 32.0
low_freq = 1.0
high_freq = 4.0
initial_context = 8192.0

BF = jnp.bfloat16
F32 = jnp.float32


def frequencies():
    half = HEAD_DIM // 2
    base_freqs = rope_base ** (-(jnp.arange(half, dtype=F32) * 2.0 / HEAD_DIM))
    wavelen = 2.0 * math.pi / base_freqs
    smooth = (initial_context / wavelen - low_freq) / (high_freq - low_freq)
    middle = (1.0 - smooth) * base_freqs / rope_scale + smooth * base_freqs
    return jnp.where(
        wavelen < initial_context / high_freq,
        base_freqs,
        jnp.where(wavelen > initial_context / low_freq, base_freqs / rope_scale, middle),
    )


def angles_of(positions):
    turned = positions.astype(F32)[:, None] * frequencies()[None, :]
    return (jnp.cos(turned)[:, None, :], jnp.sin(turned)[:, None, :])


def rotate(values, cosine, sine):
    half = values.shape[-1] // 2
    first, second = values[..., :half], values[..., half:]
    return jnp.concatenate(
        [first * cosine - second * sine, second * cosine + first * sine], axis=-1
    )


def product(left, right):
    return jnp.dot(left, right, preferred_element_type=F32)


def product_t(left, right):
    return jnp.einsum("rc,dc->rd", left, right, preferred_element_type=F32)


def contract_rows(left, right):
    return jnp.einsum("ra,rb->ab", left, right, preferred_element_type=F32)


def norm_of(values):
    factor = lax.rsqrt(jnp.mean(values * values, axis=-1, keepdims=True) + epsilon)
    return (values * factor, factor)


def norm_backward(grad_hat, normed, factor):
    return factor * (grad_hat - normed * jnp.mean(grad_hat * normed, axis=-1, keepdims=True))


def pick(array, index, axis):
    return lax.dynamic_index_in_dim(array, index, axis, keepdims=False)


def put(buffer, block, *places):
    shape, start = list(buffer.shape), [0] * buffer.ndim
    for axis, index in places:
        shape[axis], start[axis] = 1, index
    return lax.dynamic_update_slice(buffer, block.reshape(shape), start)


def after(value, *others):
    return lax.optimization_barrier((value, *others))[0]


class Grid:
    def __init__(self):
        batch, seq = lax.axis_size("batch"), lax.axis_size("seq")
        self.cn, self.zn = 2, 4
        self.yn, self.xn = batch // self.cn, seq // self.zn
        b, s = lax.axis_index("batch"), lax.axis_index("seq")
        self.y, self.c = b // self.cn, b % self.cn
        self.z, self.x = s // self.xn, s % self.xn
        self.sizes = (self.yn, self.cn, self.zn, self.xn)

    def send(self, value, y=0, c=0, z=0, x=0):
        yn, cn, zn, xn = self.sizes
        pairs = []
        for i in range(yn * cn * zn * xn):
            here = (i // (cn * zn * xn), i // (zn * xn) % cn, i // xn % zn, i % xn)
            there = (here[0] ^ y, here[1] ^ c, here[2] ^ z, here[3] ^ x)
            pairs.append((i, ((there[0] * cn + there[1]) * zn + there[2]) * xn + there[3]))
        return lax.ppermute(value, ("batch", "seq"), pairs)

    def plane(self):
        return [(ky, kx) for ky in range(self.yn) for kx in range(self.xn) if ky or kx]


def attention_weights(grid, packed):
    rows, _, cols = packed.shape
    yn, cn, zn, xn = grid.sizes
    mine = jnp.zeros((yn, xn, rows, cols), BF)
    mine = put(mine, pick(packed, grid.y * xn + grid.x, 1), (0, grid.y), (1, grid.x))
    for ky, kx in grid.plane():
        there = (grid.y ^ ky) * xn + (grid.x ^ kx)
        got = grid.send(pick(packed, there, 1), y=ky, x=kx)
        mine = put(mine, got, (0, grid.y ^ ky), (1, grid.x ^ kx))
    full = jnp.zeros((yn, cn, zn, xn, rows, cols), BF)
    for kz in range(zn):
        block = grid.send(mine, z=kz) if kz else mine
        full = put(full, block, (1, grid.c), (2, grid.z ^ kz))
        full = put(full, grid.send(block, c=1), (1, grid.c ^ 1), (2, grid.z ^ kz))
    return full.reshape(-1, cols)


def attention_grads(grid, partial):
    yn, cn, zn, xn = grid.sizes
    cols = partial.shape[1]
    partial = partial.reshape(yn, cn, zn, xn, -1, cols)
    got = grid.send(pick(partial, grid.c ^ 1, 1).astype(BF), c=1)
    total = pick(partial, grid.c, 1) + got.astype(F32)
    mine = pick(total, grid.z, 1)
    for kz in range(1, zn):
        mine = mine + grid.send(pick(total, grid.z ^ kz, 1).astype(BF), z=kz).astype(F32)
    mine = mine.astype(BF)
    rows = mine.shape[2]
    result = jnp.zeros((rows, yn * xn, cols), BF)
    result = put(result, pick(pick(mine, grid.y, 0), grid.x, 0), (1, grid.y * xn + grid.x))
    for ky, kx in grid.plane():
        got = grid.send(pick(pick(mine, grid.y ^ ky, 0), grid.x ^ kx, 0), y=ky, x=kx)
        result = put(result, got, (1, (grid.y ^ ky) * xn + (grid.x ^ kx)))
    return result.astype(F32)


def ffn_weights_near(grid, weight):
    yn, cn, zn, xn = grid.sizes
    rows = weight.shape[0]
    weight = weight.reshape(rows, zn, cn, -1)
    cols = weight.shape[3]
    both = jnp.zeros((cn, rows, zn, cols), BF)
    both = put(both, pick(weight, grid.c, 2), (0, grid.c))
    both = put(both, grid.send(pick(weight, grid.c ^ 1, 2), c=1), (0, grid.c ^ 1))
    near = jnp.zeros((cn, zn, rows, cols), BF)
    for kz in range(zn):
        block = pick(both, grid.z ^ kz, 2)
        near = put(near, grid.send(block, z=kz) if kz else block, (1, grid.z ^ kz))
    return near


def ffn_weights_far(grid, near):
    yn, cn, zn, xn = grid.sizes
    _, _, rows, cols = near.shape
    half = cols // 2
    full = jnp.zeros((yn, cn, zn, xn, rows, cols), BF)
    full = put(full, near, (0, grid.y), (3, grid.x))
    over_x = {kx: grid.send(near, x=kx) for kx in range(1, xn)}
    over_y = {ky: grid.send(near, y=ky) for ky in range(1, yn)}
    for kx, got in over_x.items():
        full = put(full, got, (0, grid.y), (3, grid.x ^ kx))
    for ky, got in over_y.items():
        full = put(full, got, (0, grid.y ^ ky), (3, grid.x))
    for ky in over_y:
        for kx in over_x:
            low = grid.send(over_x[kx][..., :half], y=ky)
            high = grid.send(over_y[ky][..., half:], x=kx)
            both = jnp.concatenate([low, high], axis=-1)
            full = put(full, both, (0, grid.y ^ ky), (3, grid.x ^ kx))
    return full.reshape(-1, cols)


def ffn_grads(grid, partial):
    yn, cn, zn, xn = grid.sizes
    cols = partial.shape[1]
    half = cols // 2
    partial = partial.reshape(yn, cn, zn, xn, -1, cols)

    def sum_x(part, axis):
        total = pick(part, grid.x, axis).astype(F32)
        for kx in range(1, xn):
            total = total + grid.send(pick(part, grid.x ^ kx, axis), x=kx).astype(F32)
        return total.astype(BF)

    def sum_y(part):
        total = pick(part, grid.y, 0).astype(F32)
        for ky in range(1, yn):
            total = total + grid.send(pick(part, grid.y ^ ky, 0), y=ky).astype(F32)
        return total.astype(BF)

    low = sum_y(sum_x(partial[..., :half], 3))
    high = sum_x(sum_y(partial[..., half:]), 2)
    mine = jnp.concatenate([low, high], axis=-1)
    rows = mine.shape[2]
    wide = jnp.zeros((cn, rows, zn, cols), BF)
    for kz in range(zn):
        block = pick(mine, grid.z ^ kz, 1)
        wide = put(wide, grid.send(block, z=kz) if kz else block, (2, grid.z ^ kz))
    result = jnp.zeros((rows, zn, cn, cols), BF)
    result = put(result, pick(wide, grid.c, 0), (2, grid.c))
    result = put(result, grid.send(pick(wide, grid.c ^ 1, 0), c=1), (2, grid.c ^ 1))
    return result.reshape(rows, zn * cn * cols).astype(F32)


def gather_plane(grid, block):
    full = jnp.zeros((grid.yn, grid.xn) + block.shape, block.dtype)
    full = put(full, block, (0, grid.y), (1, grid.x))
    for ky, kx in grid.plane():
        full = put(full, grid.send(block, y=ky, x=kx), (0, grid.y ^ ky), (1, grid.x ^ kx))
    return full


def scatter_plane(grid, partial):
    total = pick(pick(partial, grid.y, 0), grid.x, 0)
    for ky, kx in grid.plane():
        block = pick(pick(partial, grid.y ^ ky, 0), grid.x ^ kx, 0).astype(BF)
        total = total + grid.send(block, y=ky, x=kx).astype(F32)
    return total


def exchange_z(grid, blocks):
    out = jnp.zeros_like(blocks)
    for kz in range(grid.zn):
        block = pick(blocks, grid.z ^ kz, 0)
        out = put(out, grid.send(block, z=kz) if kz else block, (0, grid.z ^ kz))
    return out


def gather_column(grid, block):
    own = [grid.send(block, z=kz) if kz else block for kz in range(grid.zn)]
    other = [grid.send(part, c=1) for part in own]
    return jnp.concatenate(own + other, axis=0)


def scatter_column(grid, near, far):
    total = near + grid.send(far.astype(BF), c=1).astype(F32)
    result = total[0]
    for kz in range(1, grid.zn):
        result = result + grid.send(total[kz].astype(BF), z=kz).astype(F32)
    return result


def causal_scores(query_block, keys, offset):
    scores = (
        jnp.einsum("qehd,ked->ehqk", query_block, keys, preferred_element_type=F32)
        * HEAD_DIM ** (-0.5)
    )
    row_ids = offset + jnp.arange(query_block.shape[0], dtype=jnp.int32)
    col_ids = jnp.arange(keys.shape[0], dtype=jnp.int32)
    return jnp.where(col_ids[None, :] <= row_ids[:, None], scores, -1e30)


def attention_forward(queries, keys, values):
    length = queries.shape[0]
    block_rows = min(512, length)

    def block(index):
        offset = index * block_rows
        scores = causal_scores(
            lax.dynamic_slice_in_dim(queries, offset, block_rows, 0), keys, offset
        )
        peak = jnp.max(scores, axis=-1, keepdims=True)
        expd = jnp.exp(scores - peak)
        totals = jnp.sum(expd, axis=-1, keepdims=True)
        probs = (expd / totals).astype(BF)
        attended = jnp.einsum("ehqk,ked->qehd", probs, values, preferred_element_type=F32)
        return (attended.astype(BF), (peak + jnp.log(totals))[..., 0])

    attended, logsums = lax.map(block, jnp.arange(length // block_rows, dtype=jnp.int32))
    return (attended.reshape(length, -1), logsums)


def attention_backward(queries, keys, values, grads, logsums):
    length = queries.shape[0]
    block_rows = min(512, length)
    scale = HEAD_DIM ** (-0.5)

    def block(carry, index):
        key_sum, value_sum = carry
        offset = index * block_rows
        query_block = lax.dynamic_slice_in_dim(queries, offset, block_rows, 0)
        grad_block = lax.dynamic_slice_in_dim(grads, offset, block_rows, 0)
        scores = causal_scores(query_block, keys, offset)
        probs = jnp.exp(scores - logsums[index][..., None])
        probs_low = probs.astype(BF)
        grad_probs = jnp.einsum("qehd,ked->ehqk", grad_block, values, preferred_element_type=F32)
        centred = jnp.sum(probs * grad_probs, axis=-1, keepdims=True)
        grad_scores = (probs * (grad_probs - centred)).astype(BF)
        grad_query = (
            jnp.einsum("ehqk,ked->qehd", grad_scores, keys, preferred_element_type=F32) * scale
        ).astype(BF)
        key_sum = key_sum + scale * jnp.einsum(
            "ehqk,qehd->ked", grad_scores, query_block, preferred_element_type=F32
        )
        value_sum = value_sum + jnp.einsum(
            "ehqk,qehd->ked", probs_low, grad_block, preferred_element_type=F32
        )
        return ((key_sum, value_sum), grad_query)

    zeros = jnp.zeros(keys.shape, F32)
    (key_sum, value_sum), grad_queries = lax.scan(
        block, (zeros, zeros), jnp.arange(length // block_rows, dtype=jnp.int32)
    )
    return (grad_queries.reshape(queries.shape), key_sum.astype(BF), value_sum.astype(BF))


def body(
    inputs,
    positions,
    attn_gain,
    q_weight,
    k_weight,
    v_weight,
    o_weight,
    ffn_gain,
    gate_weight,
    up_weight,
    down_weight,
    cotangent,
):
    grid = Grid()
    yn, cn, zn, xn = grid.sizes
    _, span, width = inputs.shape
    slices = yn * xn
    expanded = max(KV_HEADS, 2 * slices)
    copies = expanded // KV_HEADS
    rows = q_weight.shape[0]
    halves = zn // yn
    q_cols = HEADS * HEAD_DIM // (slices * halves)
    kv_cols = expanded * HEAD_DIM // (slices * halves)
    part_cols = q_cols + 2 * kv_cols
    kv_part = kv_cols // HEAD_DIM
    per_kv = q_cols // kv_cols
    length = zn * xn * span

    gain_one = attn_gain.astype(F32)[:, None]
    gain_two = ffn_gain.astype(F32)[:, None]

    def widen(weight):
        return jnp.repeat(weight.reshape(rows, KV_HEADS, HEAD_DIM), copies, axis=1)

    def parts(weight, cols):
        return weight.reshape(rows, slices, halves, cols)

    wide_k, wide_v = widen(k_weight), widen(v_weight)
    qkv_rows = jnp.concatenate(
        [parts(q_weight, q_cols), parts(wide_k, kv_cols), parts(wide_v, kv_cols)], axis=3
    ).reshape(rows, slices, halves * part_cols)
    qkv_scaled = (qkv_rows.astype(F32) * gain_one[:, :, None]).astype(BF)
    gate_scaled = (gate_weight.astype(F32) * gain_two).astype(BF)
    up_scaled = (up_weight.astype(F32) * gain_two).astype(BF)

    states = inputs.reshape(span, width).astype(F32)
    unit_one, factor_one = norm_of(states)
    unit_one_low = unit_one.astype(BF)
    tokens_one = gather_plane(grid, unit_one_low).reshape(-1, width)
    qkv_full = attention_weights(grid, qkv_scaled)
    o_full = attention_weights(
        grid, o_weight.reshape(rows, slices, halves * q_cols)
    )

    spots = jnp.zeros((yn, xn, span), jnp.int32)
    spots = gather_plane(grid, positions.reshape(span))
    spots = exchange_z(grid, jnp.repeat(spots, halves, axis=0).reshape(zn, xn * span))
    cosine, sine = angles_of(spots.reshape(length))

    projected = product(tokens_one, qkv_full).reshape(
        yn, xn * span, halves, part_cols
    )
    heads_cos, heads_sin = None, None
    plane_spots = gather_plane(grid, positions.reshape(span)).reshape(yn * xn * span)
    plane_cos, plane_sin = angles_of(plane_spots)
    turn = (projected[..., : q_cols + kv_cols]).reshape(yn * xn * span, -1, HEAD_DIM)
    turned = rotate(turn, plane_cos, plane_sin).astype(BF)
    turned = turned.reshape(yn, xn * span, halves, q_cols + kv_cols)
    packed = jnp.concatenate([turned, projected[..., q_cols + kv_cols :].astype(BF)], axis=3)
    packed = packed.transpose(0, 2, 1, 3).reshape(zn, xn * span, part_cols)
    heads_in = exchange_z(grid, packed).reshape(length, part_cols)
    queries = heads_in[:, :q_cols].reshape(length, kv_part, per_kv, HEAD_DIM)
    keys = heads_in[:, q_cols : q_cols + kv_cols].reshape(length, kv_part, HEAD_DIM)
    values = heads_in[:, q_cols + kv_cols :].reshape(length, kv_part, HEAD_DIM)

    attended, logsums = attention_forward(queries, keys, values)

    def to_tokens(heads, cols):
        back = exchange_z(grid, heads.reshape(zn, xn * span, cols))
        back = back.reshape(yn, halves, xn * span, cols).transpose(0, 2, 1, 3)
        return back.reshape(yn * xn * span, halves * cols)

    attn_tokens = to_tokens(attended, q_cols)
    hidden_one = states + scatter_plane(
        grid, product_t(attn_tokens, o_full).reshape(yn, xn, span, width)
    )

    near = [ffn_weights_near(grid, w) for w in (gate_scaled, up_scaled, down_weight)]
    gate_full, up_full, down_full = [ffn_weights_far(grid, n) for n in near]
    grad_low = cotangent.reshape(span, width)
    grad_out = grad_low.astype(F32)
    grad_tokens = gather_column(grid, grad_low)
    unit_two, factor_two = norm_of(hidden_one)
    tokens_two = gather_column(grid, unit_two.astype(BF))
    gate_act = product(tokens_two, gate_full)
    up_act = product(tokens_two, up_full)
    sigmoid_gate = jax.nn.sigmoid(gate_act)
    silu_gate = gate_act * sigmoid_gate
    hidden_low = (silu_gate * up_act).astype(BF)
    grad_hidden = product(grad_tokens, down_full)
    grad_gate = (
        grad_hidden * up_act * sigmoid_gate * (1.0 + gate_act * (1.0 - sigmoid_gate))
    ).astype(BF)
    grad_up = (grad_hidden * silu_gate).astype(BF)
    grad_unit = product_t(grad_gate, gate_full) + product_t(grad_up, up_full)
    grad_unit = grad_unit.reshape(cn, zn, span, width)
    grad_hat = scatter_column(grid, grad_unit[0], grad_unit[1])
    grad_one = grad_out + norm_backward(grad_hat, unit_two, factor_two)
    result = product_t(hidden_low, down_full).reshape(cn, zn, span, width)
    output = (hidden_one + scatter_column(grid, result[0], result[1])).astype(BF)

    gate_sum = ffn_grads(grid, contract_rows(tokens_two, grad_gate).astype(BF))
    up_sum = ffn_grads(grid, contract_rows(tokens_two, grad_up).astype(BF))
    down_grad = ffn_grads(grid, contract_rows(grad_tokens, hidden_low).astype(BF))
    gate_grad = gate_sum * gain_two
    up_grad = up_sum * gain_two
    ffn_gain_grad = jnp.sum(
        gate_sum * gate_weight.astype(F32) + up_sum * up_weight.astype(F32), axis=1
    )

    branch_tokens = gather_plane(grid, grad_one.astype(BF)).reshape(-1, width)
    grad_attn = product(branch_tokens, o_full).astype(BF)
    o_sum = attention_grads(grid, contract_rows(branch_tokens, attn_tokens))
    grad_attn = grad_attn.reshape(yn, xn * span, halves, q_cols).transpose(0, 2, 1, 3)
    grad_heads = exchange_z(grid, grad_attn.reshape(zn, xn * span, q_cols))
    grad_queries, grad_keys, grad_values = attention_backward(
        queries, keys, values, grad_heads.reshape(queries.shape), logsums
    )
    heads_out = jnp.concatenate(
        [
            grad_queries.reshape(length, q_cols),
            grad_keys.reshape(length, kv_cols),
            grad_values.reshape(length, kv_cols),
        ],
        axis=1,
    )
    turn = heads_out[:, : q_cols + kv_cols].astype(F32).reshape(length, -1, HEAD_DIM)
    turned = rotate(turn, cosine, -sine).astype(BF).reshape(length, q_cols + kv_cols)
    heads_out = jnp.concatenate([turned, heads_out[:, q_cols + kv_cols :]], axis=1)
    grad_qkv = to_tokens(heads_out, part_cols)
    grad_hat_one = scatter_plane(
        grid, product_t(grad_qkv, qkv_full).reshape(yn, xn, span, width)
    )
    input_grad = grad_one + norm_backward(grad_hat_one, unit_one, factor_one)
    qkv_sum = attention_grads(grid, contract_rows(tokens_one, grad_qkv))
    attn_gain_grad = jnp.sum(qkv_sum * qkv_rows.astype(F32), axis=(1, 2))
    qkv_grad = (qkv_sum * gain_one[:, :, None]).reshape(rows, slices, halves, part_cols)

    def narrow(part):
        part = part.reshape(rows, KV_HEADS, copies, HEAD_DIM).sum(axis=2)
        return part.reshape(rows, KV_HEADS * HEAD_DIM)

    q_grad = qkv_grad[..., :q_cols].reshape(rows, HEADS * HEAD_DIM)
    k_grad = narrow(qkv_grad[..., q_cols : q_cols + kv_cols])
    v_grad = narrow(qkv_grad[..., q_cols + kv_cols :])
    return (
        output.reshape(1, span, width),
        input_grad.reshape(1, span, width),
        attn_gain_grad,
        q_grad,
        k_grad,
        v_grad,
        o_sum.reshape(rows, HEADS * HEAD_DIM),
        ffn_gain_grad,
        gate_grad,
        up_grad,
        down_grad,
    )


def solution(mesh):
    tokens = P("batch", "seq", None)
    rows = P(("batch", "seq"), None)
    gain = P(("batch", "seq"))
    return jax.shard_map(
        body,
        mesh=mesh,
        in_specs=(
            tokens, P("batch", "seq"), gain, rows, rows, rows, rows, gain, rows, rows, rows, tokens
        ),
        out_specs=(tokens, tokens, gain, rows, rows, rows, rows, gain, rows, rows, rows),
        check_vma=False,
    )
```

```python
import functools
import math

import jax
import jax.numpy as jnp
import numpy as np
from jax import lax
from jax.experimental import pallas as pl
from jax.experimental.pallas import tpu as pltpu
from jax.sharding import Mesh, PartitionSpec as P

HEADS = 32
KV_HEADS = 8
HEAD_DIM = 64

epsilon = 1e-05
rope_base = 500000.0
rope_scale = 32.0
low_freq = 1.0
high_freq = 4.0
initial_context = 8192.0

BF = jnp.bfloat16
F32 = jnp.float32


def frequencies():
    half = HEAD_DIM // 2
    base_freqs = rope_base ** (-(jnp.arange(half, dtype=F32) * 2.0 / HEAD_DIM))
    wavelen = 2.0 * math.pi / base_freqs
    smooth = (initial_context / wavelen - low_freq) / (high_freq - low_freq)
    middle = (1.0 - smooth) * base_freqs / rope_scale + smooth * base_freqs
    return jnp.where(
        wavelen < initial_context / high_freq,
        base_freqs,
        jnp.where(wavelen > initial_context / low_freq, base_freqs / rope_scale, middle),
    )


def angles_of(positions):
    turned = positions.astype(F32)[:, None] * frequencies()[None, :]
    return (jnp.cos(turned), jnp.sin(turned))


def contract_rows(left, right):
    return jnp.einsum("ra,rb->ab", left, right, preferred_element_type=F32)


def product_t(left, right):
    return jnp.einsum("rc,dc->rd", left, right, preferred_element_type=F32)


def product(left, right):
    return jnp.dot(left, right, preferred_element_type=F32)


def norm_of(values):
    factor = lax.rsqrt(jnp.mean(values * values, axis=-1, keepdims=True) + epsilon)
    return (values * factor, factor)


def norm_backward(grad_hat, normed, factor):
    return factor * (grad_hat - normed * jnp.mean(grad_hat * normed, axis=-1, keepdims=True))


def pick(array, index, axis):
    return lax.dynamic_index_in_dim(array, index, axis, keepdims=False)


def put(buffer, block, *places):
    shape, start = list(buffer.shape), [0] * buffer.ndim
    for axis, index in places:
        shape[axis], start[axis] = 1, index
    return lax.dynamic_update_slice(buffer, block.reshape(shape), start)


def after(value, *others):
    zero = jnp.zeros((), value.dtype)
    for array in others:
        first = array[(0,) * array.ndim]
        zero = zero + (first != first).astype(value.dtype)
    corner = value[tuple(slice(0, min(n, 16 if i < value.ndim - 1 else 128)) if i >= value.ndim - 2
                         else slice(0, 1) for i, n in enumerate(value.shape))]
    return lax.dynamic_update_slice(value, corner + zero, (0,) * value.ndim)


PLANE = ("y", "x")
COLUMN = ("c", "z")


def place(axes):
    return lax.axis_index(axes), lax.axis_size(axes)


def trade(value, axes, step):
    count = lax.axis_size(axes)
    return lax.ppermute(value, axes, [(i, i ^ step) for i in range(count)])


def swap(blocks, axes, at=0):
    here, count = place(axes)
    return [pick(blocks, here, at)] + [
        trade(pick(blocks, here ^ k, at), axes, k) for k in range(1, count)
    ]


def spread(block, axes):
    count = lax.axis_size(axes)
    return [block] + [trade(block, axes, k) for k in range(1, count)]


def in_order(blocks, axes):
    here, count = place(axes)
    out = jnp.zeros((count,) + blocks[0].shape, blocks[0].dtype)
    for k, block in enumerate(blocks):
        out = put(out, block, (0, here ^ k))
    return out


def total(blocks):
    result = blocks[0].astype(F32)
    for block in blocks[1:]:
        result = result + block.astype(F32)
    return result


def order_kernel(order, group, in_ref, out_ref):
    wide = max(group, 128)
    for at in range(0, out_ref.shape[1], wide):
        first = at // group
        parts = [
            in_ref[:, j * group : (j + 1) * group] for j in order[first : first + wide // group]
        ]
        out_ref[:, at : at + wide] = jnp.concatenate(parts, axis=1).astype(out_ref.dtype)


def reorder(features, sizes, before, dtype):
    later = "yxcz" if before == "yczx" else "yczx"
    count = math.prod(sizes.values())
    axes = np.arange(count).reshape([sizes[axis] for axis in before])
    order = axes.transpose([before.index(axis) for axis in later]).reshape(-1).tolist()
    return in_vmem(
        functools.partial(order_kernel, order, features.shape[1] // count),
        [features],
        [jax.ShapeDtypeStruct(features.shape, dtype)],
        [],
        0,
    )[0]


def attention_weights(mine, sizes, splits):
    yn, cn, zn, xn = [sizes[axis] for axis in "yczx"]
    rows = mine.shape[1]
    core, column = lax.axis_index("c"), lax.axis_index("z")
    own = spread(mine, "z")
    results = []
    for start, end in splits:
        full = jnp.zeros((yn * xn, cn, zn, rows, end - start), BF)
        for k in range(zn):
            full = put(full, own[k][..., start:end], (1, core), (2, column ^ k))
        other = trade(pick(full, core, 1), "c", 1)
        results.append(put(full, other, (1, core ^ 1)).reshape(-1, end - start))
    return results, own[1:]


def attention_grads(partial, sizes, *earlier):
    yn, cn, zn, xn = [sizes[axis] for axis in "yczx"]
    cols = partial.shape[-1]
    blocks = partial.reshape(yn * xn, cn, zn, -1, cols)
    core = lax.axis_index("c")
    got = trade(pick(blocks, core ^ 1, 1).astype(BF), "c", 1)
    near = (pick(blocks, core, 1) + got.astype(F32)).astype(BF)
    there = swap(after(near, *earlier), "z", 1)
    mine = total(there).astype(BF)
    return in_order(swap(mine, PLANE), PLANE).astype(F32), there[1:]


def all_to_all(blocks, axes):
    return lax.all_to_all(blocks, axes, split_axis=0, concat_axis=0, tiled=True)


def ffn_weights_near(weights, sizes):
    slices = sizes["c"] * sizes["z"]
    split = [w.reshape(w.shape[0], slices, -1).transpose(1, 0, 2) for w in weights]
    return all_to_all(jnp.concatenate(split, axis=2), COLUMN)


def ffn_weights_far(near):
    full = lax.all_gather(near, PLANE, axis=0, tiled=False)
    return full.reshape(-1, near.shape[-1])


def ffn_grads(partial, sizes):
    cols = partial.shape[-1]
    blocks = partial.reshape(sizes["y"] * sizes["x"], -1, cols)
    mine = lax.psum_scatter(blocks, PLANE, scatter_dimension=0, tiled=False)
    return mine.reshape(sizes["c"], sizes["z"], -1, cols)


def ffn_grads_near(mine, *earlier):
    core, column = lax.axis_index("c"), lax.axis_index("z")
    own = pick(mine, core, 0)
    other = after(trade(pick(mine, core ^ 1, 0), "c", 1), *earlier)
    parts = []
    for k in range(mine.shape[1]):
        part = jnp.stack([pick(own, column ^ k, 0), pick(other, column ^ k, 0)])
        parts.append(trade(part, "z", k) if k else part)
    return parts


def ffn_slices(sizes):
    core, column = lax.axis_index("c"), lax.axis_index("z")
    spots = [
        other * sizes["z"] + (column ^ k) for k in range(sizes["z"]) for other in (core, core ^ 1)
    ]
    return jnp.stack(spots).astype(jnp.int32)


def scatter_plane(partial):
    return total(list(all_to_all(partial, PLANE)))


def gather(block, axes):
    copies = jnp.broadcast_to(block, (lax.axis_size(axes),) + block.shape)
    return all_to_all(copies, axes)


VMEM_BYTES = 56 * 1024 * 1024
TILE = 256
NT = (((1,), (1,)), ((), ()))


def mm(left, right):
    return jnp.dot(left, right, preferred_element_type=F32)


def mm_nt(left, right):
    return lax.dot_general(left, right, NT, preferred_element_type=F32)


def causal(scores, start, tile):
    keys = lax.broadcasted_iota(jnp.int32, (tile, tile), 0)
    queries = lax.broadcasted_iota(jnp.int32, (tile, tile), 1)
    last = jnp.where(keys <= queries, scores[start:], -1e30)
    return last if start == 0 else jnp.concatenate([scores[:start], last], axis=0)


def forward_kernel(q_cols, kv_cols, seq, result, logsums):
    length = seq.shape[0]
    tile = min(TILE, length)
    per_kv = q_cols // kv_cols
    for e in range(kv_cols // HEAD_DIM):
        at = q_cols + e * HEAD_DIM
        keys = seq[:, at : at + HEAD_DIM]
        at = q_cols + kv_cols + e * HEAD_DIM
        values_t = seq[:, at : at + HEAD_DIM].T
        for start in range(0, length, tile):
            end = start + tile
            turned = []
            for h in range(e * per_kv, (e + 1) * per_kv):
                queries = seq[start:end, h * HEAD_DIM : (h + 1) * HEAD_DIM]
                scores = causal(mm_nt(keys[:end], queries) * HEAD_DIM ** (-0.5), start, tile)
                peak = jnp.max(scores, axis=0, keepdims=True)
                expd = jnp.exp(scores - peak)
                sums = jnp.sum(expd, axis=0, keepdims=True)
                logsums[h : h + 1, start:end] = peak + jnp.log(sums)
                probs = (expd * (1.0 / sums)).astype(BF)
                turned.append(mm(values_t[:, :end], probs))
            at = e * per_kv * HEAD_DIM
            result[start:end, at : at + per_kv * HEAD_DIM] = (
                jnp.concatenate(turned, axis=0).T.astype(BF)
            )


def backward_kernel(q_cols, kv_cols, seq, grads, logsums, result, key_sum, value_sum):
    length = seq.shape[0]
    tile = min(TILE, length)
    per_kv = q_cols // kv_cols
    scale = HEAD_DIM ** (-0.5)
    for e in range(kv_cols // HEAD_DIM):
        key_at = q_cols + e * HEAD_DIM
        value_at = q_cols + kv_cols + e * HEAD_DIM
        keys = seq[:, key_at : key_at + HEAD_DIM]
        keys_t = keys.T
        values = seq[:, value_at : value_at + HEAD_DIM]
        key_sum[...] = jnp.zeros_like(key_sum)
        value_sum[...] = jnp.zeros_like(value_sum)
        for start in range(0, length, tile):
            end = start + tile
            turned = []
            for h in range(e * per_kv, (e + 1) * per_kv):
                at = h * HEAD_DIM
                queries = seq[start:end, at : at + HEAD_DIM]
                grad = grads[start:end, at : at + HEAD_DIM]
                scores = causal(mm_nt(keys[:end], queries) * scale, start, tile)
                probs = jnp.exp(scores - logsums[h : h + 1, start:end])
                grad_probs = mm_nt(values[:end], grad)
                centred = jnp.sum(probs * grad_probs, axis=0, keepdims=True)
                grad_scores = (probs * (grad_probs - centred)).astype(BF)
                value_sum[:end, :] += mm(probs.astype(BF), grad)
                key_sum[:end, :] += mm(grad_scores, queries)
                turned.append(mm(keys_t[:, :end], grad_scores))
            at = e * per_kv * HEAD_DIM
            result[start:end, at : at + per_kv * HEAD_DIM] = (
                jnp.concatenate(turned, axis=0).T * scale
            ).astype(BF)
        result[:, key_at : key_at + HEAD_DIM] = (key_sum[...] * scale).astype(BF)
        result[:, value_at : value_at + HEAD_DIM] = value_sum[...].astype(BF)


def turn(values, cosine, sine, rotated):
    lane = lax.broadcasted_iota(jnp.int32, cosine.shape, 1)
    first_half = lane % HEAD_DIM < HEAD_DIM // 2
    parts = []
    for tile in range(values.shape[1] // 128):
        part = values[:, tile * 128 : (tile + 1) * 128]
        low, high = rotated[2 * tile], rotated[2 * tile + 1]
        if low or high:
            left = pltpu.roll(part, 128 - HEAD_DIM // 2, 1)
            right = pltpu.roll(part, HEAD_DIM // 2, 1)
            moved = part * cosine + jnp.where(first_half, left, right) * sine
            if low and high:
                part = moved
            else:
                part = jnp.where((lane < HEAD_DIM) == low, moved, part)
        parts.append(part)
    return jnp.concatenate(parts, axis=1)


def qkv_kernel(halves, rotated, x_ref, w_ref, cosine, sine, out_ref):
    piece, part = out_ref.shape[1:]
    for y in range(out_ref.shape[0] // halves):
        rows = pl.ds(y * piece, piece)
        values = mm(x_ref[rows, : w_ref.shape[0]], w_ref[...])
        values = turn(values, cosine[rows, :], sine[rows, :], rotated).astype(BF)
        for h in range(halves):
            out_ref[y * halves + h] = values[:, h * part : (h + 1) * part]


def qkv_back_kernel(halves, rotated, blocks, w_ref, cosine, sine, grad_ref, out_ref):
    count, piece = blocks.shape[:2]
    for y in range(count // halves):
        rows = pl.ds(y * piece, piece)
        values = jnp.concatenate([blocks[y * halves + h] for h in range(halves)], axis=1)
        values = turn(values.astype(F32), cosine[rows, :], -sine[rows, :], rotated).astype(BF)
        grad_ref[rows, :] = values
        part = mm_nt(values, w_ref[...]).astype(BF)
        for x in range(piece // out_ref.shape[1]):
            out_ref[y * (piece // out_ref.shape[1]) + x] = part[
                x * out_ref.shape[1] : (x + 1) * out_ref.shape[1]
            ]


def o_kernel(halves, blocks, w_ref, tokens_ref, out_ref):
    count, piece = blocks.shape[:2]
    for y in range(count // halves):
        rows = pl.ds(y * piece, piece)
        values = jnp.concatenate([blocks[y * halves + h] for h in range(halves)], axis=1)
        tokens_ref[rows, :] = values
        part = mm_nt(values, w_ref[...]).astype(BF)
        for x in range(piece // out_ref.shape[1]):
            out_ref[y * (piece // out_ref.shape[1]) + x] = part[
                x * out_ref.shape[1] : (x + 1) * out_ref.shape[1]
            ]


def ffn_kernel(tiles, *refs):
    x_ref, dy_ref, gate_ref, up_ref, down_ref, gate_rows, up_rows = refs[:7]
    z_ref, dgate_ref, dup_ref, dx_ref, held_gate, held_up = refs[7:]
    step = pl.program_id(0)
    tile = gate_ref.shape[1]
    for i in range(tiles):

        @pl.when(step == i)
        def _():
            gate = mm(x_ref[...], gate_ref[...])
            up = mm(x_ref[...], up_ref[...])
            dz = mm(dy_ref[...], down_ref[...])
            sigmoid = jax.nn.sigmoid(gate)
            silu = gate * sigmoid
            z_ref[...] = (silu * up).astype(BF)
            dgate = (dz * up * sigmoid * (1.0 + gate * (1.0 - sigmoid))).astype(BF)
            dup = (dz * silu).astype(BF)
            dgate_ref[...] = dgate
            dup_ref[...] = dup
            held_gate[:, i * tile : (i + 1) * tile] = dgate
            held_up[:, i * tile : (i + 1) * tile] = dup

    @pl.when(step >= tiles)
    def _():
        part = mm_nt(held_gate[...], gate_rows[...]) + mm_nt(held_up[...], up_rows[...])
        dx_ref[...] = part.astype(dx_ref.dtype)


def ffn(tokens, grads, weights, out_dtype):
    count, width = tokens.shape
    units = weights.shape[1] // 3
    tile, row_tile = min(256, units), min(1024, width)
    tiles, row_tiles = units // tile, width // row_tile

    def first(i):
        return jnp.minimum(i, tiles - 1)

    def second(i):
        return jnp.maximum(i - tiles, 0)

    whole = pl.BlockSpec((count, width), lambda i: (0, 0))
    narrow = pl.BlockSpec((count, tile), lambda i: (0, first(i)))
    columns = [
        pl.BlockSpec((width, tile), lambda i, j=j: (0, j * tiles + first(i))) for j in range(3)
    ]
    across = [pl.BlockSpec((row_tile, units), lambda i, j=j: (second(i), j)) for j in range(2)]
    hidden = jax.ShapeDtypeStruct((count, units), BF)
    return pl.pallas_call(
        functools.partial(ffn_kernel, tiles),
        grid=(tiles + row_tiles,),
        out_shape=[hidden] * 3 + [jax.ShapeDtypeStruct((count, width), out_dtype)],
        in_specs=[whole, whole] + columns + across,
        out_specs=[narrow] * 3 + [pl.BlockSpec((count, row_tile), lambda i: (0, second(i)))],
        scratch_shapes=[pltpu.VMEM((count, units), BF)] * 2,
        compiler_params=pltpu.CompilerParams(vmem_limit_bytes=VMEM_BYTES),
        cost_estimate=pl.CostEstimate(flops=1, bytes_accessed=1, transcendentals=0),
    )(tokens, grads, *[weights] * 5)


def add_product_kernel(z_ref, down_ref, *refs):
    part = mm_nt(z_ref[...], down_ref[...])
    for held in refs[:-1]:
        part = part + held[...].astype(F32)
    refs[-1][...] = part.astype(BF)


def add_product(z, weights, *added):
    count, units = z.shape
    width = weights.shape[0]
    tile = min(512, width)
    part = pl.BlockSpec((count, tile), lambda i: (0, i))
    return pl.pallas_call(
        add_product_kernel,
        grid=(width // tile,),
        out_shape=jax.ShapeDtypeStruct((count, width), BF),
        in_specs=[
            pl.BlockSpec((count, units), lambda i: (0, 0)),
            pl.BlockSpec((tile, units), lambda i: (i, 2)),
        ]
        + [part] * len(added),
        out_specs=part,
        compiler_params=pltpu.CompilerParams(vmem_limit_bytes=VMEM_BYTES),
        cost_estimate=pl.CostEstimate(flops=1, bytes_accessed=1, transcendentals=0),
    )(z, weights, *added)


def outer_kernel(count, *refs):
    left_near, left_far = refs[0][...].T, refs[1][...].T
    outs = refs[2 + 2 * count :]
    for j in range(count):
        near, far = refs[2 + 2 * j], refs[3 + 2 * j]
        outs[0][:, j * near.shape[1] : (j + 1) * near.shape[1]] = (
            mm(left_near, near[...]) + mm(left_far, far[...])
        ).astype(BF)


def outer(left, rights):
    count, width = left[0].shape
    units = rights[0][0].shape[1]
    tile = min(512, width)
    flat = [array for pair in rights for array in pair]
    return pl.pallas_call(
        functools.partial(outer_kernel, len(rights)),
        grid=(width // tile,),
        out_shape=[jax.ShapeDtypeStruct((width, len(rights) * units), BF)],
        in_specs=[pl.BlockSpec((count, tile), lambda i: (0, i))] * 2
        + [pl.BlockSpec((count, units), lambda i: (0, 0))] * len(flat),
        out_specs=[pl.BlockSpec((tile, len(rights) * units), lambda i: (i, 0))],
        compiler_params=pltpu.CompilerParams(vmem_limit_bytes=VMEM_BYTES),
        cost_estimate=pl.CostEstimate(flops=1, bytes_accessed=1, transcendentals=0),
    )(*left, *flat)[0]


def finish_kernel(count, slices, *refs):
    pieces = len(refs) - 2 * count - 3
    spots, parts = refs[0], refs[1 : 1 + pieces]
    weights, gain = refs[1 + pieces : 1 + pieces + count], refs[1 + pieces + count]
    outs, gain_out = refs[2 + pieces + count : -1], refs[-1]
    width = outs[0].shape[1] // slices
    found = 0.0
    for k in range(pieces):
        for i in range(parts[k].shape[0]):
            spot = spots[k * parts[k].shape[0] + i]
            columns = pl.ds(pl.multiple_of(spot * width, width), width)
            for j in range(count):
                part = parts[k][i, :, j * width : (j + 1) * width].astype(F32)
                outs[j][:, columns] = part * gain[...]
                found = found + part * weights[j][:, columns].astype(F32)
    gain_out[...] = jnp.sum(found, axis=1, keepdims=True)


def finish(parts, spots, weights, gain):
    count, rows = len(weights), weights[0].shape[0]
    return in_vmem(
        functools.partial(finish_kernel, count, sum(part.shape[0] for part in parts)),
        list(parts) + list(weights) + [gain],
        [jax.ShapeDtypeStruct(weight.shape, F32) for weight in weights]
        + [jax.ShapeDtypeStruct((rows, 1), F32)],
        [],
        4 * math.prod(weights[0].shape) * count,
        spots,
    )


def in_vmem(kernel, operands, outs, scratch, flops, places=None):
    moved = sum(math.prod(array.shape) * 2 for array in list(operands) + outs)
    first = [] if places is None else [places]
    return pl.pallas_call(
        kernel,
        out_shape=outs,
        in_specs=[pl.BlockSpec(memory_space=pltpu.SMEM)] * len(first)
        + kernel_specs(len(operands)),
        out_specs=kernel_specs(len(outs)),
        scratch_shapes=scratch,
        compiler_params=pltpu.CompilerParams(vmem_limit_bytes=VMEM_BYTES),
        cost_estimate=pl.CostEstimate(flops=1, bytes_accessed=1, transcendentals=0),
    )(*first, *operands)


def kernel_specs(count):
    return [pl.BlockSpec(memory_space=pltpu.VMEM)] * count


def attention_forward(seq, q_cols, kv_cols):
    length = seq.shape[0]
    scores = (q_cols // HEAD_DIM) * length * length // 2
    return in_vmem(
        functools.partial(forward_kernel, q_cols, kv_cols),
        [seq],
        [
            jax.ShapeDtypeStruct((length, q_cols), BF),
            jax.ShapeDtypeStruct((q_cols // HEAD_DIM, length), F32),
        ],
        [],
        scores * HEAD_DIM * 16,
    )


def attention_backward(seq, grads, logsums, q_cols, kv_cols):
    length = seq.shape[0]
    scores = (q_cols // HEAD_DIM) * length * length // 2
    return in_vmem(
        functools.partial(backward_kernel, q_cols, kv_cols),
        [seq, grads, logsums],
        [jax.ShapeDtypeStruct(seq.shape, BF)],
        [pltpu.VMEM((length, HEAD_DIM), F32)] * 2,
        scores * HEAD_DIM * 40,
    )[0]


def body(
    inputs,
    positions,
    attn_gain,
    q_weight,
    k_weight,
    v_weight,
    o_weight,
    ffn_gain,
    gate_weight,
    up_weight,
    down_weight,
    cotangent,
):
    sizes = {axis: lax.axis_size(axis) for axis in "yczx"}
    yn, cn, zn, xn = [sizes[axis] for axis in "yczx"]
    _, span, width = inputs.shape
    slices = yn * xn
    expanded = max(KV_HEADS, 2 * slices)
    copies = expanded // KV_HEADS
    rows = q_weight.shape[0]
    halves = zn // yn
    q_cols = HEADS * HEAD_DIM // (slices * halves)
    kv_cols = expanded * HEAD_DIM // (slices * halves)
    part_cols = q_cols + 2 * kv_cols
    piece = xn * span
    length = zn * piece

    states = reorder(inputs.reshape(span, width), sizes, "yczx", F32)
    grad_low = reorder(cotangent.reshape(span, width), sizes, "yczx", BF)

    gain_one = attn_gain.astype(F32)[:, None]
    gain_two = ffn_gain.astype(F32)[:, None]

    def widen(weight):
        return jnp.repeat(weight.reshape(rows, KV_HEADS, HEAD_DIM), copies, axis=1)

    def parts(weight, cols):
        return weight.reshape(rows, slices, halves, cols)

    wide_k, wide_v = widen(k_weight), widen(v_weight)
    qkv_rows = (
        jnp.concatenate(
            [parts(q_weight, q_cols), parts(wide_k, kv_cols), parts(wide_v, kv_cols)], axis=3
        )
        .reshape(rows, slices, halves * part_cols)
        .transpose(1, 0, 2)
    )
    qkv_scaled = (qkv_rows.astype(F32) * gain_one[None]).astype(BF)
    gate_scaled = (gate_weight.astype(F32) * gain_two).astype(BF)
    up_scaled = (up_weight.astype(F32) * gain_two).astype(BF)

    unit_one, factor_one = norm_of(states)
    o_rows = o_weight.reshape(rows, slices, halves * q_cols).transpose(1, 0, 2)
    near_attn = in_order(swap(jnp.concatenate([qkv_scaled, o_rows], axis=2), PLANE), PLANE)
    ffn_near = ffn_weights_near((gate_scaled, up_scaled, down_weight), sizes)
    digits = jnp.stack([positions.reshape(span) // 128, positions.reshape(span) % 128], axis=1)
    digits = jnp.repeat(digits.astype(BF), HEAD_DIM, axis=1)
    tokens_one = lax.all_gather(
        jnp.concatenate([unit_one.astype(BF), digits], axis=1), PLANE, axis=0, tiled=True
    )
    ffn_full = ffn_weights_far(after(ffn_near, near_attn))
    qkv_width = halves * part_cols
    (qkv_full, o_full), qkv_there = attention_weights(
        after(near_attn, ffn_near), sizes, ((0, qkv_width), (qkv_width, near_attn.shape[-1]))
    )
    digits = tokens_one[:, width:].astype(F32)
    cosine, sine = angles_of(digits[:, 0] * 128.0 + digits[:, HEAD_DIM])
    cosine = jnp.concatenate([cosine] * 4, axis=1)
    sine = jnp.concatenate([-sine, sine] * 2, axis=1)
    rotated = ([True] * ((q_cols + kv_cols) // HEAD_DIM) + [False] * (kv_cols // HEAD_DIM)) * halves
    count = slices * span
    attn_flops = 2 * count * width * halves * part_cols

    (packed,) = in_vmem(
        functools.partial(qkv_kernel, halves, rotated),
        [tokens_one, qkv_full, cosine, sine],
        [jax.ShapeDtypeStruct((zn, piece, part_cols), BF)],
        [],
        attn_flops,
    )
    heads_in = all_to_all(packed, "z").reshape(length, part_cols)
    attended, logsums = attention_forward(heads_in, q_cols, kv_cols)
    grad_steps = [trade(after(grad_low, heads_in), "z", k) for k in range(1, zn)]
    attended = after(attended, grad_steps[0])
    attended = all_to_all(attended.reshape(zn, piece, q_cols), "z")

    attn_tokens, o_part = in_vmem(
        functools.partial(o_kernel, halves),
        [attended, o_full],
        [
            jax.ShapeDtypeStruct((count, halves * q_cols), BF),
            jax.ShapeDtypeStruct((slices, span, width), BF),
        ],
        [],
        2 * count * width * halves * q_cols,
    )
    hidden_one = after(states + scatter_plane(o_part), ffn_full, *grad_steps[1:])

    grad_out = grad_low.astype(F32)
    grad_near = in_order([after(grad_low, hidden_one)] + grad_steps, "z")
    grad_far = trade(grad_near, "c", 1)
    unit_two, factor_two = norm_of(hidden_one)
    tokens_near = gather(unit_two.astype(BF), "z")
    tokens_far = trade(tokens_near, "c", 1)
    tokens_near, tokens_far, grad_near, grad_far = [
        array.reshape(-1, width) for array in (tokens_near, tokens_far, grad_near, grad_far)
    ]
    z_near, dgate_near, dup_near, dx_near = ffn(tokens_near, grad_near, ffn_full, F32)
    z_far, dgate_far, dup_far, dx_far = ffn(tokens_far, grad_far, ffn_full, BF)
    blocks = (zn, span, width)
    down_part = outer((grad_near, grad_far), [(z_near, z_far)])
    grad_both = dx_near.reshape(blocks) + trade(dx_far.reshape(blocks), "c", 1).astype(F32)
    grad_both = grad_both.astype(BF)
    grad_there = all_to_all(grad_both, "z")
    grad_hat = total(list(grad_there))
    gate_up_part = outer(
        (tokens_near, tokens_far),
        [(dgate_near, dgate_far), (dup_near, dup_far)],
    )
    result_far = add_product(z_far, ffn_full)
    result_near = add_product(z_near, ffn_full, trade(result_far, "c", 1)).reshape(blocks)
    grad_hat = after(grad_hat, result_near, gate_up_part, down_part)
    grad_one = grad_out + norm_backward(grad_hat, unit_two, factor_two)
    result_there = swap(after(result_near, grad_one), "z")
    down_sum = ffn_grads(after(down_part, grad_both), sizes)
    branch_tokens = gather(grad_one.astype(BF), PLANE).reshape(-1, width)
    branch_tokens = after(branch_tokens, *result_there[1:3])
    gate_up_sum = ffn_grads(after(gate_up_part, branch_tokens), sizes)
    grad_attn = product(branch_tokens, o_full).astype(BF)
    grad_attn = grad_attn.reshape(yn, piece, halves, q_cols).transpose(0, 2, 1, 3)
    grad_heads = all_to_all(grad_attn.reshape(zn, piece, q_cols), "z")
    down_sum = ffn_grads_near(down_sum)
    grad_heads = grad_heads.reshape(length, q_cols)
    heads_out = attention_backward(heads_in, grad_heads, logsums, q_cols, kv_cols)
    heads_out = after(heads_out, *down_sum[1:3])
    back = all_to_all(heads_out.reshape(zn, piece, part_cols), "z")
    o_sum, o_sum_there = attention_grads(
        contract_rows(branch_tokens, after(attn_tokens, heads_out)), sizes, back
    )
    gate_up_sum = ffn_grads_near(gate_up_sum, heads_out)
    output = (after(hidden_one, grad_heads) + total(result_there)).astype(BF)
    grad_qkv, hat_part = in_vmem(
        functools.partial(qkv_back_kernel, halves, rotated),
        [back, qkv_full, cosine, sine],
        [
            jax.ShapeDtypeStruct((count, halves * part_cols), BF),
            jax.ShapeDtypeStruct((slices, span, width), BF),
        ],
        [],
        attn_flops,
    )
    grad_hat_one = after(scatter_plane(hat_part), result_there[3], down_sum[3])
    input_grad = grad_one + norm_backward(grad_hat_one, unit_one, factor_one)
    qkv_sum, _ = attention_grads(
        contract_rows(tokens_one[:, :width], grad_qkv), sizes
    )
    attn_gain_grad = jnp.sum(qkv_sum * qkv_rows.astype(F32), axis=(0, 2))
    qkv_grad = (qkv_sum * gain_one[None]).transpose(1, 0, 2)
    qkv_grad = qkv_grad.reshape(rows, slices, halves, part_cols)
    spots = ffn_slices(sizes)
    gate_grad, up_grad, ffn_gain_grad = finish(
        gate_up_sum, spots, (gate_weight, up_weight), gain_two
    )
    (down_grad, _) = finish(down_sum, spots, (down_weight,), jnp.ones_like(gain_two))

    def narrow(part):
        part = part.reshape(rows, KV_HEADS, copies, HEAD_DIM).sum(axis=2)
        return part.reshape(rows, KV_HEADS * HEAD_DIM)

    q_grad = qkv_grad[..., :q_cols].reshape(rows, HEADS * HEAD_DIM)
    k_grad = narrow(qkv_grad[..., q_cols : q_cols + kv_cols])
    v_grad = narrow(qkv_grad[..., q_cols + kv_cols :])
    return (
        reorder(output, sizes, "yxcz", BF).reshape(1, span, width),
        reorder(input_grad, sizes, "yxcz", F32).reshape(1, span, width),
        attn_gain_grad,
        q_grad,
        k_grad,
        v_grad,
        o_sum.transpose(1, 0, 2).reshape(rows, HEADS * HEAD_DIM),
        ffn_gain_grad.reshape(rows),
        gate_grad,
        up_grad,
        down_grad,
    )


def solution(mesh):
    batch, seq = mesh.devices.shape
    cores, column = 2, 4
    parts = mesh.devices.reshape(batch // cores, cores, column, seq // column)
    tokens = P(("y", "c"), ("z", "x"), None)
    rows = P(("y", "c", "z", "x"), None)
    gain = P(("y", "c", "z", "x"))
    return jax.shard_map(
        body,
        mesh=Mesh(parts, ("y", "c", "z", "x")),
        in_specs=(
            tokens, P(("y", "c"), ("z", "x")), gain, rows, rows, rows, rows, gain, rows, rows, rows,
            tokens,
        ),
        out_specs=(tokens, tokens, gain, rows, rows, rows, rows, gain, rows, rows, rows),
        check_vma=False,
    )
```

```python
import functools
import math

import jax
import jax.numpy as jnp
import numpy as np
from jax import lax
from jax.experimental import pallas as pl
from jax.experimental.pallas import tpu as pltpu
from jax.sharding import Mesh, PartitionSpec as P

HEADS = 32
KV_HEADS = 8
HEAD_DIM = 64

epsilon = 1e-05
rope_base = 500000.0
rope_scale = 32.0
low_freq = 1.0
high_freq = 4.0
initial_context = 8192.0

BF = jnp.bfloat16
F32 = jnp.float32


def frequencies():
    half = HEAD_DIM // 2
    base_freqs = rope_base ** (-(jnp.arange(half, dtype=F32) * 2.0 / HEAD_DIM))
    wavelen = 2.0 * math.pi / base_freqs
    smooth = (initial_context / wavelen - low_freq) / (high_freq - low_freq)
    middle = (1.0 - smooth) * base_freqs / rope_scale + smooth * base_freqs
    return jnp.where(
        wavelen < initial_context / high_freq,
        base_freqs,
        jnp.where(wavelen > initial_context / low_freq, base_freqs / rope_scale, middle),
    )


def angles_of(positions):
    turned = positions.astype(F32)[:, None] * frequencies()[None, :]
    return (jnp.cos(turned), jnp.sin(turned))


def contract_rows(left, right):
    return jnp.einsum("ra,rb->ab", left, right, preferred_element_type=F32)


def product_t(left, right):
    return jnp.einsum("rc,dc->rd", left, right, preferred_element_type=F32)


def product(left, right):
    return jnp.dot(left, right, preferred_element_type=F32)


def norm_of(values):
    factor = lax.rsqrt(jnp.mean(values * values, axis=-1, keepdims=True) + epsilon)
    return (values * factor, factor)


def norm_backward(grad_hat, normed, factor):
    return factor * (grad_hat - normed * jnp.mean(grad_hat * normed, axis=-1, keepdims=True))


def pick(array, index, axis):
    return lax.dynamic_index_in_dim(array, index, axis, keepdims=False)


def put(buffer, block, *places):
    shape, start = list(buffer.shape), [0] * buffer.ndim
    for axis, index in places:
        shape[axis], start[axis] = 1, index
    return lax.dynamic_update_slice(buffer, block.reshape(shape), start)


def after(value, *others):
    zero = jnp.zeros((), value.dtype)
    for array in others:
        first = array[(0,) * array.ndim]
        zero = zero + (first != first).astype(value.dtype)
    corner = value[tuple(slice(0, min(n, 16 if i < value.ndim - 1 else 128)) if i >= value.ndim - 2
                         else slice(0, 1) for i, n in enumerate(value.shape))]
    return lax.dynamic_update_slice(value, corner + zero, (0,) * value.ndim)


PLANE = ("y", "x")
COLUMN = ("c", "z")


def place(axes):
    return lax.axis_index(axes), lax.axis_size(axes)


def trade(value, axes, step):
    count = lax.axis_size(axes)
    return lax.ppermute(value, axes, [(i, i ^ step) for i in range(count)])


def swap(blocks, axes, at=0):
    here, count = place(axes)
    return [pick(blocks, here, at)] + [
        trade(pick(blocks, here ^ k, at), axes, k) for k in range(1, count)
    ]


def spread(block, axes):
    count = lax.axis_size(axes)
    return [block] + [trade(block, axes, k) for k in range(1, count)]


def in_order(blocks, axes):
    here, count = place(axes)
    out = jnp.zeros((count,) + blocks[0].shape, blocks[0].dtype)
    for k, block in enumerate(blocks):
        out = put(out, block, (0, here ^ k))
    return out


def total(blocks):
    result = blocks[0].astype(F32)
    for block in blocks[1:]:
        result = result + block.astype(F32)
    return result


def order_kernel(order, group, in_ref, out_ref):
    wide = max(group, 128)
    for at in range(0, out_ref.shape[1], wide):
        first = at // group
        parts = [
            in_ref[:, j * group : (j + 1) * group] for j in order[first : first + wide // group]
        ]
        out_ref[:, at : at + wide] = jnp.concatenate(parts, axis=1).astype(out_ref.dtype)


def reorder(features, sizes, before, dtype):
    later = "yxcz" if before == "yczx" else "yczx"
    count = math.prod(sizes.values())
    axes = np.arange(count).reshape([sizes[axis] for axis in before])
    order = axes.transpose([before.index(axis) for axis in later]).reshape(-1).tolist()
    return in_vmem(
        functools.partial(order_kernel, order, features.shape[1] // count),
        [features],
        [jax.ShapeDtypeStruct(features.shape, dtype)],
        [],
    )[0]


def attention_weights(mine, sizes, splits):
    yn, cn, zn, xn = [sizes[axis] for axis in "yczx"]
    rows = mine.shape[1]
    core, column = lax.axis_index("c"), lax.axis_index("z")
    own = spread(mine, "z")
    results = []
    for start, end in splits:
        full = jnp.zeros((yn * xn, cn, zn, rows, end - start), BF)
        for k in range(zn):
            full = put(full, own[k][..., start:end], (1, core), (2, column ^ k))
        other = trade(pick(full, core, 1), "c", 1)
        results.append(put(full, other, (1, core ^ 1)).reshape(-1, end - start))
    return results, own[1:]


def attention_grads(partial, sizes, *earlier):
    yn, cn, zn, xn = [sizes[axis] for axis in "yczx"]
    cols = partial.shape[-1]
    blocks = partial.reshape(yn * xn, cn, zn, -1, cols)
    core = lax.axis_index("c")
    got = trade(pick(blocks, core ^ 1, 1).astype(BF), "c", 1)
    near = (pick(blocks, core, 1) + got.astype(F32)).astype(BF)
    there = swap(after(near, *earlier), "z", 1)
    mine = total(there).astype(BF)
    return in_order(swap(mine, PLANE), PLANE).astype(F32), there[1:]


def all_to_all(blocks, axes):
    return lax.all_to_all(blocks, axes, split_axis=0, concat_axis=0, tiled=True)


def ffn_weights_near(weights, sizes):
    slices = sizes["c"] * sizes["z"]
    split = [w.reshape(w.shape[0], slices, -1).transpose(1, 0, 2) for w in weights]
    return all_to_all(jnp.concatenate(split, axis=2), COLUMN)


def ffn_weights_far(near):
    full = lax.all_gather(near, PLANE, axis=0, tiled=False)
    return full.reshape(-1, near.shape[-1])


def ffn_grads(partial, sizes):
    cols = partial.shape[-1]
    blocks = partial.reshape(sizes["y"] * sizes["x"], -1, cols)
    mine = lax.psum_scatter(blocks, PLANE, scatter_dimension=0, tiled=False)
    return mine.reshape(sizes["c"], sizes["z"], -1, cols)


def ffn_grads_near(mine, *earlier):
    core, column = lax.axis_index("c"), lax.axis_index("z")
    own = pick(mine, core, 0)
    other = after(trade(pick(mine, core ^ 1, 0), "c", 1), *earlier)
    parts = []
    for k in range(mine.shape[1]):
        part = jnp.stack([pick(own, column ^ k, 0), pick(other, column ^ k, 0)])
        parts.append(trade(part, "z", k) if k else part)
    return parts


def ffn_slices(sizes):
    core, column = lax.axis_index("c"), lax.axis_index("z")
    spots = [
        other * sizes["z"] + (column ^ k) for k in range(sizes["z"]) for other in (core, core ^ 1)
    ]
    return jnp.stack(spots).astype(jnp.int32)


def scatter_plane(partial):
    return total(list(all_to_all(partial, PLANE)))


def gather(block, axes):
    copies = jnp.broadcast_to(block, (lax.axis_size(axes),) + block.shape)
    return all_to_all(copies, axes)


VMEM_BYTES = 56 * 1024 * 1024
TILE = 256
NT = (((1,), (1,)), ((), ()))


def mm(left, right):
    return jnp.dot(left, right, preferred_element_type=F32)


def mm_nt(left, right):
    return lax.dot_general(left, right, NT, preferred_element_type=F32)


def causal(scores, start, tile):
    keys = lax.broadcasted_iota(jnp.int32, (tile, tile), 0)
    queries = lax.broadcasted_iota(jnp.int32, (tile, tile), 1)
    last = jnp.where(keys <= queries, scores[start:], -1e30)
    return last if start == 0 else jnp.concatenate([scores[:start], last], axis=0)


def forward_kernel(q_cols, kv_cols, seq, result, logsums):
    length = seq.shape[0]
    tile = min(TILE, length)
    per_kv = q_cols // kv_cols
    for e in range(kv_cols // HEAD_DIM):
        at = q_cols + e * HEAD_DIM
        keys = seq[:, at : at + HEAD_DIM]
        at = q_cols + kv_cols + e * HEAD_DIM
        values_t = seq[:, at : at + HEAD_DIM].T
        for start in range(0, length, tile):
            end = start + tile
            turned = []
            for h in range(e * per_kv, (e + 1) * per_kv):
                queries = seq[start:end, h * HEAD_DIM : (h + 1) * HEAD_DIM]
                scores = causal(mm_nt(keys[:end], queries) * HEAD_DIM ** (-0.5), start, tile)
                peak = jnp.max(scores, axis=0, keepdims=True)
                expd = jnp.exp(scores - peak)
                sums = jnp.sum(expd, axis=0, keepdims=True)
                logsums[h : h + 1, start:end] = peak + jnp.log(sums)
                probs = (expd * (1.0 / sums)).astype(BF)
                turned.append(mm(values_t[:, :end], probs))
            at = e * per_kv * HEAD_DIM
            result[start:end, at : at + per_kv * HEAD_DIM] = (
                jnp.concatenate(turned, axis=0).T.astype(BF)
            )


def backward_kernel(q_cols, kv_cols, seq, grads, logsums, result, key_sum, value_sum):
    length = seq.shape[0]
    tile = min(TILE, length)
    per_kv = q_cols // kv_cols
    scale = HEAD_DIM ** (-0.5)
    for e in range(kv_cols // HEAD_DIM):
        key_at = q_cols + e * HEAD_DIM
        value_at = q_cols + kv_cols + e * HEAD_DIM
        keys = seq[:, key_at : key_at + HEAD_DIM]
        keys_t = keys.T
        values = seq[:, value_at : value_at + HEAD_DIM]
        key_sum[...] = jnp.zeros_like(key_sum)
        value_sum[...] = jnp.zeros_like(value_sum)
        for start in range(0, length, tile):
            end = start + tile
            turned = []
            for h in range(e * per_kv, (e + 1) * per_kv):
                at = h * HEAD_DIM
                queries = seq[start:end, at : at + HEAD_DIM]
                grad = grads[start:end, at : at + HEAD_DIM]
                scores = causal(mm_nt(keys[:end], queries) * scale, start, tile)
                probs = jnp.exp(scores - logsums[h : h + 1, start:end])
                grad_probs = mm_nt(values[:end], grad)
                centred = jnp.sum(probs * grad_probs, axis=0, keepdims=True)
                grad_scores = (probs * (grad_probs - centred)).astype(BF)
                value_sum[:end, :] += mm(probs.astype(BF), grad)
                key_sum[:end, :] += mm(grad_scores, queries)
                turned.append(mm(keys_t[:, :end], grad_scores))
            at = e * per_kv * HEAD_DIM
            result[start:end, at : at + per_kv * HEAD_DIM] = (
                jnp.concatenate(turned, axis=0).T * scale
            ).astype(BF)
        result[:, key_at : key_at + HEAD_DIM] = (key_sum[...] * scale).astype(BF)
        result[:, value_at : value_at + HEAD_DIM] = value_sum[...].astype(BF)


def turn(values, cosine, sine, rotated):
    lane = lax.broadcasted_iota(jnp.int32, cosine.shape, 1)
    first_half = lane % HEAD_DIM < HEAD_DIM // 2
    parts = []
    for tile in range(values.shape[1] // 128):
        part = values[:, tile * 128 : (tile + 1) * 128]
        low, high = rotated[2 * tile], rotated[2 * tile + 1]
        if low or high:
            left = pltpu.roll(part, 128 - HEAD_DIM // 2, 1)
            right = pltpu.roll(part, HEAD_DIM // 2, 1)
            moved = part * cosine + jnp.where(first_half, left, right) * sine
            if low and high:
                part = moved
            else:
                part = jnp.where((lane < HEAD_DIM) == low, moved, part)
        parts.append(part)
    return jnp.concatenate(parts, axis=1)


def qkv_kernel(halves, rotated, x_ref, w_ref, cosine, sine, out_ref):
    piece, part = out_ref.shape[1:]
    for y in range(out_ref.shape[0] // halves):
        rows = pl.ds(y * piece, piece)
        values = mm(x_ref[rows, : w_ref.shape[0]], w_ref[...])
        values = turn(values, cosine[rows, :], sine[rows, :], rotated).astype(BF)
        for h in range(halves):
            out_ref[y * halves + h] = values[:, h * part : (h + 1) * part]


def heads_kernel(halves, x_ref, w_ref, out_ref):
    piece, cols = out_ref.shape[1:]
    for y in range(out_ref.shape[0] // halves):
        values = mm(x_ref[pl.ds(y * piece, piece), :], w_ref[...]).astype(BF)
        for h in range(halves):
            out_ref[y * halves + h] = values[:, h * cols : (h + 1) * cols]


def summed(parts):
    result = parts[0].astype(F32)
    for i in range(1, parts.shape[0]):
        result = result + parts[i].astype(F32)
    return result


def hidden_norm_kernel(parts, states, hidden_ref, unit_ref, factor_ref, copies):
    hidden = states[...] + summed(parts)
    unit, factor = norm_of(hidden)
    hidden_ref[...] = hidden
    unit_ref[...] = unit
    factor_ref[...] = factor
    for i in range(copies.shape[0]):
        copies[i] = unit.astype(BF)


def norm_back_kernel(parts, grad_out, unit, factor, grad_ref, copies):
    back = norm_backward(summed(parts), unit[...], factor[...])
    grad = grad_out[...].astype(F32) + back
    grad_ref[...] = grad
    for i in range(copies.shape[0]):
        copies[i] = grad.astype(BF)


def qkv_back_kernel(halves, rotated, blocks, w_ref, cosine, sine, grad_ref, out_ref):
    count, piece = blocks.shape[:2]
    for y in range(count // halves):
        rows = pl.ds(y * piece, piece)
        values = jnp.concatenate([blocks[y * halves + h] for h in range(halves)], axis=1)
        values = turn(values.astype(F32), cosine[rows, :], -sine[rows, :], rotated).astype(BF)
        grad_ref[rows, :] = values
        part = mm_nt(values, w_ref[...]).astype(BF)
        for x in range(piece // out_ref.shape[1]):
            out_ref[y * (piece // out_ref.shape[1]) + x] = part[
                x * out_ref.shape[1] : (x + 1) * out_ref.shape[1]
            ]


def o_kernel(halves, blocks, w_ref, tokens_ref, out_ref):
    count, piece = blocks.shape[:2]
    for y in range(count // halves):
        rows = pl.ds(y * piece, piece)
        values = jnp.concatenate([blocks[y * halves + h] for h in range(halves)], axis=1)
        tokens_ref[rows, :] = values
        part = mm_nt(values, w_ref[...]).astype(BF)
        for x in range(piece // out_ref.shape[1]):
            out_ref[y * (piece // out_ref.shape[1]) + x] = part[
                x * out_ref.shape[1] : (x + 1) * out_ref.shape[1]
            ]


def ffn_kernel(tiles, *refs):
    x_ref, dy_ref, gate_ref, up_ref, down_ref, gate_rows, up_rows = refs[:7]
    z_ref, dgate_ref, dup_ref, dx_ref, held_gate, held_up = refs[7:]
    step = pl.program_id(0)
    tile = gate_ref.shape[1]
    for i in range(tiles):

        @pl.when(step == i)
        def _():
            gate = mm(x_ref[...], gate_ref[...])
            up = mm(x_ref[...], up_ref[...])
            dz = mm(dy_ref[...], down_ref[...])
            sigmoid = jax.nn.sigmoid(gate)
            silu = gate * sigmoid
            z_ref[...] = (silu * up).astype(BF)
            dgate = (dz * up * sigmoid * (1.0 + gate * (1.0 - sigmoid))).astype(BF)
            dup = (dz * silu).astype(BF)
            dgate_ref[...] = dgate
            dup_ref[...] = dup
            held_gate[:, i * tile : (i + 1) * tile] = dgate
            held_up[:, i * tile : (i + 1) * tile] = dup

    @pl.when(step >= tiles)
    def _():
        part = mm_nt(held_gate[...], gate_rows[...]) + mm_nt(held_up[...], up_rows[...])
        dx_ref[...] = part.astype(dx_ref.dtype)


def ffn(tokens, grads, weights, out_dtype, ties=()):
    count, width = tokens.shape
    units = weights.shape[1] // 3
    tile, row_tile = min(256, units), min(1024, width)
    tiles, row_tiles = units // tile, width // row_tile

    def first(i):
        return jnp.minimum(i, tiles - 1)

    def second(i):
        return jnp.maximum(i - tiles, 0)

    whole = pl.BlockSpec((count, width), lambda i: (0, 0))
    narrow = pl.BlockSpec((count, tile), lambda i: (0, first(i)))
    columns = [
        pl.BlockSpec((width, tile), lambda i, j=j: (0, j * tiles + first(i))) for j in range(3)
    ]
    across = [pl.BlockSpec((row_tile, units), lambda i, j=j: (second(i), j)) for j in range(2)]
    hidden = jax.ShapeDtypeStruct((count, units), BF)
    return pl.pallas_call(
        skipping(functools.partial(ffn_kernel, tiles), 7, len(ties)),
        grid=(tiles + row_tiles,),
        out_shape=[hidden] * 3 + [jax.ShapeDtypeStruct((count, width), out_dtype)],
        in_specs=[whole, whole]
        + columns
        + across
        + [pl.BlockSpec(memory_space=pl.ANY)] * len(ties),
        out_specs=[narrow] * 3 + [pl.BlockSpec((count, row_tile), lambda i: (0, second(i)))],
        scratch_shapes=[pltpu.VMEM((count, units), BF)] * 2,
        compiler_params=pltpu.CompilerParams(vmem_limit_bytes=VMEM_BYTES),
        cost_estimate=pl.CostEstimate(flops=1, bytes_accessed=1, transcendentals=0),
    )(tokens, grads, *[weights] * 5, *ties)


def add_product_kernel(z_ref, down_ref, *refs):
    part = mm_nt(z_ref[...], down_ref[...])
    for held in refs[:-1]:
        part = part + held[...].astype(F32)
    refs[-1][...] = part.astype(BF)


def add_product(z, weights, *added):
    count, units = z.shape
    width = weights.shape[0]
    tile = min(512, width)
    part = pl.BlockSpec((count, tile), lambda i: (0, i))
    return pl.pallas_call(
        add_product_kernel,
        grid=(width // tile,),
        out_shape=jax.ShapeDtypeStruct((count, width), BF),
        in_specs=[
            pl.BlockSpec((count, units), lambda i: (0, 0)),
            pl.BlockSpec((tile, units), lambda i: (i, 2)),
        ]
        + [part] * len(added),
        out_specs=part,
        compiler_params=pltpu.CompilerParams(vmem_limit_bytes=VMEM_BYTES),
        cost_estimate=pl.CostEstimate(flops=1, bytes_accessed=1, transcendentals=0),
    )(z, weights, *added)


def outer_kernel(count, *refs):
    left_near, left_far = refs[0][...].T, refs[1][...].T
    outs = refs[2 + 2 * count :]
    for j in range(count):
        near, far = refs[2 + 2 * j], refs[3 + 2 * j]
        outs[0][:, j * near.shape[1] : (j + 1) * near.shape[1]] = (
            mm(left_near, near[...]) + mm(left_far, far[...])
        ).astype(BF)


def outer(left, rights, ties=()):
    count, width = left[0].shape
    units = rights[0][0].shape[1]
    tile = min(512, width)
    flat = [array for pair in rights for array in pair]
    return pl.pallas_call(
        skipping(functools.partial(outer_kernel, len(rights)), 2 + len(flat), len(ties)),
        grid=(width // tile,),
        out_shape=[jax.ShapeDtypeStruct((width, len(rights) * units), BF)],
        in_specs=[pl.BlockSpec((count, tile), lambda i: (0, i))] * 2
        + [pl.BlockSpec((count, units), lambda i: (0, 0))] * len(flat)
        + [pl.BlockSpec(memory_space=pl.ANY)] * len(ties),
        out_specs=[pl.BlockSpec((tile, len(rights) * units), lambda i: (i, 0))],
        compiler_params=pltpu.CompilerParams(vmem_limit_bytes=VMEM_BYTES),
        cost_estimate=pl.CostEstimate(flops=1, bytes_accessed=1, transcendentals=0),
    )(*left, *flat, *ties)[0]


def finish_kernel(count, slices, *refs):
    pieces = len(refs) - 2 * count - 3
    spots, parts = refs[0], refs[1 : 1 + pieces]
    weights, gain = refs[1 + pieces : 1 + pieces + count], refs[1 + pieces + count]
    outs, gain_out = refs[2 + pieces + count : -1], refs[-1]
    width = outs[0].shape[1] // slices
    found = 0.0
    for k in range(pieces):
        for i in range(parts[k].shape[0]):
            spot = spots[k * parts[k].shape[0] + i]
            columns = pl.ds(pl.multiple_of(spot * width, width), width)
            for j in range(count):
                part = parts[k][i, :, j * width : (j + 1) * width].astype(F32)
                outs[j][:, columns] = part * gain[...]
                found = found + part * weights[j][:, columns].astype(F32)
    gain_out[...] = jnp.sum(found, axis=1, keepdims=True)


def finish(parts, spots, weights, gain):
    count, rows = len(weights), weights[0].shape[0]
    return in_vmem(
        functools.partial(finish_kernel, count, sum(part.shape[0] for part in parts)),
        list(parts) + list(weights) + [gain],
        [jax.ShapeDtypeStruct(weight.shape, F32) for weight in weights]
        + [jax.ShapeDtypeStruct((rows, 1), F32)],
        [],
        spots,
    )


def skipping(kernel, at, count):
    return lambda *refs: kernel(*refs[:at], *refs[at + count :])


def in_vmem(kernel, operands, outs, scratch, places=None, ties=()):
    first = [] if places is None else [places]
    kernel = skipping(kernel, len(first) + len(operands), len(ties))
    return pl.pallas_call(
        kernel,
        out_shape=outs,
        in_specs=[pl.BlockSpec(memory_space=pltpu.SMEM)] * len(first)
        + kernel_specs(len(operands))
        + [pl.BlockSpec(memory_space=pl.ANY)] * len(ties),
        out_specs=kernel_specs(len(outs)),
        scratch_shapes=scratch,
        compiler_params=pltpu.CompilerParams(vmem_limit_bytes=VMEM_BYTES),
        cost_estimate=pl.CostEstimate(flops=1, bytes_accessed=1, transcendentals=0),
    )(*first, *operands, *ties)


def kernel_specs(count):
    return [pl.BlockSpec(memory_space=pltpu.VMEM)] * count


def attention_forward(seq, q_cols, kv_cols):
    length = seq.shape[0]
    return in_vmem(
        functools.partial(forward_kernel, q_cols, kv_cols),
        [seq],
        [
            jax.ShapeDtypeStruct((length, q_cols), BF),
            jax.ShapeDtypeStruct((q_cols // HEAD_DIM, length), F32),
        ],
        [],
    )


def attention_backward(seq, grads, logsums, q_cols, kv_cols):
    length = seq.shape[0]
    return in_vmem(
        functools.partial(backward_kernel, q_cols, kv_cols),
        [seq, grads, logsums],
        [jax.ShapeDtypeStruct(seq.shape, BF)],
        [pltpu.VMEM((length, HEAD_DIM), F32)] * 2,
    )[0]


def body(
    inputs,
    positions,
    attn_gain,
    q_weight,
    k_weight,
    v_weight,
    o_weight,
    ffn_gain,
    gate_weight,
    up_weight,
    down_weight,
    cotangent,
):
    sizes = {axis: lax.axis_size(axis) for axis in "yczx"}
    yn, cn, zn, xn = [sizes[axis] for axis in "yczx"]
    _, span, width = inputs.shape
    slices = yn * xn
    expanded = max(KV_HEADS, 2 * slices)
    copies = expanded // KV_HEADS
    rows = q_weight.shape[0]
    halves = zn // yn
    q_cols = HEADS * HEAD_DIM // (slices * halves)
    kv_cols = expanded * HEAD_DIM // (slices * halves)
    part_cols = q_cols + 2 * kv_cols
    piece = xn * span
    length = zn * piece

    states = reorder(inputs.reshape(span, width), sizes, "yczx", F32)
    grad_low = reorder(cotangent.reshape(span, width), sizes, "yczx", BF)

    gain_one = attn_gain.astype(F32)[:, None]
    gain_two = ffn_gain.astype(F32)[:, None]

    def widen(weight):
        return jnp.repeat(weight.reshape(rows, KV_HEADS, HEAD_DIM), copies, axis=1)

    def parts(weight, cols):
        return weight.reshape(rows, slices, halves, cols)

    wide_k, wide_v = widen(k_weight), widen(v_weight)
    qkv_rows = (
        jnp.concatenate(
            [parts(q_weight, q_cols), parts(wide_k, kv_cols), parts(wide_v, kv_cols)], axis=3
        )
        .reshape(rows, slices, halves * part_cols)
        .transpose(1, 0, 2)
    )
    qkv_scaled = (qkv_rows.astype(F32) * gain_one[None]).astype(BF)
    gate_scaled = (gate_weight.astype(F32) * gain_two).astype(BF)
    up_scaled = (up_weight.astype(F32) * gain_two).astype(BF)

    unit_one, factor_one = norm_of(states)
    o_rows = o_weight.reshape(rows, slices, halves * q_cols).transpose(1, 0, 2)
    near_attn = in_order(swap(jnp.concatenate([qkv_scaled, o_rows], axis=2), PLANE), PLANE)
    ffn_near = ffn_weights_near((gate_scaled, up_scaled, down_weight), sizes)
    digits = jnp.stack([positions.reshape(span) // 128, positions.reshape(span) % 128], axis=1)
    digits = jnp.repeat(digits.astype(BF), HEAD_DIM, axis=1)
    tokens_one = lax.all_gather(
        jnp.concatenate([unit_one.astype(BF), digits], axis=1), PLANE, axis=0, tiled=True
    )
    ffn_full = ffn_weights_far(after(ffn_near, near_attn))
    qkv_width = halves * part_cols
    (qkv_full, o_full), qkv_there = attention_weights(
        after(near_attn, ffn_near), sizes, ((0, qkv_width), (qkv_width, near_attn.shape[-1]))
    )
    digits = tokens_one[:, width:].astype(F32)
    cosine, sine = angles_of(digits[:, 0] * 128.0 + digits[:, HEAD_DIM])
    cosine = jnp.concatenate([cosine] * 4, axis=1)
    sine = jnp.concatenate([-sine, sine] * 2, axis=1)
    rotated = ([True] * ((q_cols + kv_cols) // HEAD_DIM) + [False] * (kv_cols // HEAD_DIM)) * halves
    count = slices * span

    (packed,) = in_vmem(
        functools.partial(qkv_kernel, halves, rotated),
        [tokens_one, qkv_full, cosine, sine],
        [jax.ShapeDtypeStruct((zn, piece, part_cols), BF)],
        [],
    )
    heads_in = all_to_all(packed, "z").reshape(length, part_cols)
    attended, logsums = attention_forward(heads_in, q_cols, kv_cols)
    grad_near = lax.all_gather(after(grad_low, attended), "z", axis=0, tiled=False)
    attended = all_to_all(attended.reshape(zn, piece, q_cols), "z")

    attn_tokens, o_part = in_vmem(
        functools.partial(o_kernel, halves),
        [attended, o_full],
        [
            jax.ShapeDtypeStruct((count, halves * q_cols), BF),
            jax.ShapeDtypeStruct((slices, span, width), BF),
        ],
        [],
    )
    square = jax.ShapeDtypeStruct((span, width), F32)
    hidden_one, unit_two, factor_two, tokens_near = in_vmem(
        hidden_norm_kernel,
        [all_to_all(o_part, PLANE), states],
        [
            square,
            square,
            jax.ShapeDtypeStruct((span, 1), F32),
            jax.ShapeDtypeStruct((zn, span, width), BF),
        ],
        [],
        ties=[ffn_full],
    )

    grad_far = trade(grad_near, "c", 1)
    tokens_near = all_to_all(tokens_near, "z")
    tokens_far = trade(tokens_near, "c", 1)
    tokens_near, tokens_far, grad_near, grad_far = [
        array.reshape(-1, width) for array in (tokens_near, tokens_far, grad_near, grad_far)
    ]
    z_far, dgate_far, dup_far, dx_far = ffn(tokens_far, grad_far, ffn_full, BF)
    z_near, dgate_near, dup_near, dx_near = ffn(
        tokens_near, grad_near, ffn_full, F32, [dx_far]
    )
    blocks = (zn, span, width)
    grad_both = dx_near.reshape(blocks) + trade(dx_far.reshape(blocks), "c", 1).astype(F32)
    grad_both = grad_both.astype(BF)
    grad_there = all_to_all(grad_both, "z")
    gate_up_part = outer(
        (tokens_near, tokens_far),
        [(dgate_near, dgate_far), (dup_near, dup_far)],
    )
    result_far = add_product(z_far, ffn_full)
    result_near = add_product(z_near, ffn_full, trade(result_far, "c", 1)).reshape(blocks)
    down_part = outer((grad_near, grad_far), [(z_near, z_far)])
    grad_one, branch_tokens = in_vmem(
        norm_back_kernel,
        [grad_there, grad_low, unit_two, factor_two],
        [square, jax.ShapeDtypeStruct((slices, span, width), BF)],
        [],
        ties=[result_near, gate_up_part],
    )
    result_there = swap(result_near, "z")
    down_sum = ffn_grads(down_part, sizes)

    branch_tokens = all_to_all(branch_tokens, PLANE).reshape(-1, width)
    (grad_attn,) = in_vmem(
        functools.partial(heads_kernel, halves),
        [branch_tokens, o_full],
        [jax.ShapeDtypeStruct((zn, piece, q_cols), BF)],
        [],
        ties=result_there[1:3],
    )
    gate_up_sum = ffn_grads(after(gate_up_part, grad_attn), sizes)
    grad_heads = all_to_all(grad_attn, "z")
    down_sum = ffn_grads_near(down_sum)
    grad_heads = grad_heads.reshape(length, q_cols)
    heads_out = attention_backward(heads_in, grad_heads, logsums, q_cols, kv_cols)
    back = all_to_all(heads_out.reshape(zn, piece, part_cols), "z")
    o_sum, o_sum_there = attention_grads(
        contract_rows(branch_tokens, attn_tokens), sizes, back
    )
    gate_up_sum = ffn_grads_near(gate_up_sum)
    output = (after(hidden_one, grad_heads) + total(result_there)).astype(BF)
    grad_qkv, hat_part = in_vmem(
        functools.partial(qkv_back_kernel, halves, rotated),
        [back, qkv_full, cosine, sine],
        [
            jax.ShapeDtypeStruct((count, halves * part_cols), BF),
            jax.ShapeDtypeStruct((slices, span, width), BF),
        ],
        [],
        ties=down_sum[1:],
    )
    grad_hat_one = after(scatter_plane(hat_part), result_there[3])
    input_grad = grad_one + norm_backward(grad_hat_one, unit_one, factor_one)
    qkv_sum, _ = attention_grads(
        contract_rows(tokens_one[:, :width], grad_qkv), sizes
    )
    attn_gain_grad = jnp.sum(qkv_sum * qkv_rows.astype(F32), axis=(0, 2))
    qkv_grad = (qkv_sum * gain_one[None]).transpose(1, 0, 2)
    qkv_grad = qkv_grad.reshape(rows, slices, halves, part_cols)
    spots = ffn_slices(sizes)
    gate_grad, up_grad, ffn_gain_grad = finish(
        gate_up_sum, spots, (gate_weight, up_weight), gain_two
    )
    (down_grad, _) = finish(down_sum, spots, (down_weight,), jnp.ones_like(gain_two))

    def narrow(part):
        part = part.reshape(rows, KV_HEADS, copies, HEAD_DIM).sum(axis=2)
        return part.reshape(rows, KV_HEADS * HEAD_DIM)

    q_grad = qkv_grad[..., :q_cols].reshape(rows, HEADS * HEAD_DIM)
    k_grad = narrow(qkv_grad[..., q_cols : q_cols + kv_cols])
    v_grad = narrow(qkv_grad[..., q_cols + kv_cols :])
    return (
        reorder(output, sizes, "yxcz", BF).reshape(1, span, width),
        reorder(input_grad, sizes, "yxcz", F32).reshape(1, span, width),
        attn_gain_grad,
        q_grad,
        k_grad,
        v_grad,
        o_sum.transpose(1, 0, 2).reshape(rows, HEADS * HEAD_DIM),
        ffn_gain_grad.reshape(rows),
        gate_grad,
        up_grad,
        down_grad,
    )


def solution(mesh):
    batch, seq = mesh.devices.shape
    cores, column = 2, 4
    parts = mesh.devices.reshape(batch // cores, cores, column, seq // column)
    tokens = P(("y", "c"), ("z", "x"), None)
    rows = P(("y", "c", "z", "x"), None)
    gain = P(("y", "c", "z", "x"))
    return jax.shard_map(
        body,
        mesh=Mesh(parts, ("y", "c", "z", "x")),
        in_specs=(
            tokens, P(("y", "c"), ("z", "x")), gain, rows, rows, rows, rows, gain, rows, rows, rows,
            tokens,
        ),
        out_specs=(tokens, tokens, gain, rows, rows, rows, rows, gain, rows, rows, rows),
        check_vma=False,
    )
```

```python
import functools
import math

import jax
import jax.numpy as jnp
import numpy as np
from jax import lax
from jax.experimental import pallas as pl
from jax.experimental.pallas import tpu as pltpu
from jax.sharding import Mesh, PartitionSpec as P

HEADS = 32
KV_HEADS = 8
HEAD_DIM = 64

epsilon = 1e-05
rope_base = 500000.0
rope_scale = 32.0
low_freq = 1.0
high_freq = 4.0
initial_context = 8192.0

BF = jnp.bfloat16
F32 = jnp.float32


def frequencies():
    half = HEAD_DIM // 2
    base_freqs = rope_base ** (-(jnp.arange(half, dtype=F32) * 2.0 / HEAD_DIM))
    wavelen = 2.0 * math.pi / base_freqs
    smooth = (initial_context / wavelen - low_freq) / (high_freq - low_freq)
    middle = (1.0 - smooth) * base_freqs / rope_scale + smooth * base_freqs
    return jnp.where(
        wavelen < initial_context / high_freq,
        base_freqs,
        jnp.where(wavelen > initial_context / low_freq, base_freqs / rope_scale, middle),
    )


def angles_of(positions):
    turned = positions.astype(F32)[:, None] * frequencies()[None, :]
    return (jnp.cos(turned), jnp.sin(turned))


def contract_rows(left, right):
    return jnp.einsum("ra,rb->ab", left, right, preferred_element_type=F32)


def product_t(left, right):
    return jnp.einsum("rc,dc->rd", left, right, preferred_element_type=F32)


def product(left, right):
    return jnp.dot(left, right, preferred_element_type=F32)


def norm_of(values):
    factor = lax.rsqrt(jnp.mean(values * values, axis=-1, keepdims=True) + epsilon)
    return (values * factor, factor)


def norm_backward(grad_hat, normed, factor):
    return factor * (grad_hat - normed * jnp.mean(grad_hat * normed, axis=-1, keepdims=True))


def pick(array, index, axis):
    return lax.dynamic_index_in_dim(array, index, axis, keepdims=False)


def put(buffer, block, *places):
    shape, start = list(buffer.shape), [0] * buffer.ndim
    for axis, index in places:
        shape[axis], start[axis] = 1, index
    return lax.dynamic_update_slice(buffer, block.reshape(shape), start)


def after(value, *others):
    zero = jnp.zeros((), value.dtype)
    for array in others:
        first = array[(0,) * array.ndim]
        zero = zero + (first != first).astype(value.dtype)
    corner = value[tuple(slice(0, min(n, 16 if i < value.ndim - 1 else 128)) if i >= value.ndim - 2
                         else slice(0, 1) for i, n in enumerate(value.shape))]
    return lax.dynamic_update_slice(value, corner + zero, (0,) * value.ndim)


PLANE = ("y", "x")
COLUMN = ("c", "z")


def place(axes):
    return lax.axis_index(axes), lax.axis_size(axes)


def trade(value, axes, step):
    count = lax.axis_size(axes)
    return lax.ppermute(value, axes, [(i, i ^ step) for i in range(count)])


def swap(blocks, axes, at=0):
    here, count = place(axes)
    return [pick(blocks, here, at)] + [
        trade(pick(blocks, here ^ k, at), axes, k) for k in range(1, count)
    ]


def spread(block, axes):
    count = lax.axis_size(axes)
    return [block] + [trade(block, axes, k) for k in range(1, count)]


def in_order(blocks, axes):
    here, count = place(axes)
    out = jnp.zeros((count,) + blocks[0].shape, blocks[0].dtype)
    for k, block in enumerate(blocks):
        out = put(out, block, (0, here ^ k))
    return out


def total(blocks):
    result = blocks[0].astype(F32)
    for block in blocks[1:]:
        result = result + block.astype(F32)
    return result


def order_kernel(order, group, in_ref, out_ref):
    wide = max(group, 128)
    for at in range(0, out_ref.shape[1], wide):
        first = at // group
        parts = [
            in_ref[:, j * group : (j + 1) * group] for j in order[first : first + wide // group]
        ]
        out_ref[:, at : at + wide] = jnp.concatenate(parts, axis=1).astype(out_ref.dtype)


def reorder(features, sizes, before, dtype):
    later = "yxcz" if before == "yczx" else "yczx"
    count = math.prod(sizes.values())
    axes = np.arange(count).reshape([sizes[axis] for axis in before])
    order = axes.transpose([before.index(axis) for axis in later]).reshape(-1).tolist()
    return in_vmem(
        functools.partial(order_kernel, order, features.shape[1] // count),
        [features],
        [jax.ShapeDtypeStruct(features.shape, dtype)],
        [],
    )[0]


def attention_weights(own, sizes):
    yn, cn, zn, xn = [sizes[axis] for axis in "yczx"]
    rows, cols = own[0].shape[1:]
    core, column = lax.axis_index("c"), lax.axis_index("z")
    full = jnp.zeros((yn * xn, cn, zn, rows, cols), BF)
    for k in range(zn):
        full = put(full, own[k], (1, core), (2, column ^ k))
    other = trade(pick(full, core, 1), "c", 1)
    return put(full, other, (1, core ^ 1)).reshape(-1, cols)


def attention_grads(partial, sizes, earlier, later):
    yn, cn, zn, xn = [sizes[axis] for axis in "yczx"]
    cols = partial.shape[-1]
    blocks = partial.reshape(yn * xn, cn, zn, -1, cols)
    core = lax.axis_index("c")
    got = trade(pick(blocks, core ^ 1, 1).astype(BF), "c", 1)
    near = (pick(blocks, core, 1) + got.astype(F32)).astype(BF)
    there = swap(after(near, *earlier), "z", 1)
    mine = after(total(there).astype(BF), *later)
    return in_order(swap(mine, PLANE), PLANE).astype(F32), there[1:]


def all_to_all(blocks, axes):
    return lax.all_to_all(blocks, axes, split_axis=0, concat_axis=0, tiled=True)


def ffn_weights_near(weights, sizes):
    slices = sizes["c"] * sizes["z"]
    split = [w.reshape(w.shape[0], slices, -1).transpose(1, 0, 2) for w in weights]
    return all_to_all(jnp.concatenate(split, axis=2), COLUMN)


def ffn_weights_far(near):
    full = lax.all_gather(near, PLANE, axis=0, tiled=False)
    return full.reshape(-1, near.shape[-1])


def ffn_grads(partial, sizes):
    cols = partial.shape[-1]
    blocks = partial.reshape(sizes["y"] * sizes["x"], -1, cols)
    mine = lax.psum_scatter(blocks, PLANE, scatter_dimension=0, tiled=False)
    return mine.reshape(sizes["c"], sizes["z"], -1, cols)


def ffn_grads_near(mine):
    core, column = lax.axis_index("c"), lax.axis_index("z")
    own = pick(mine, core, 0)
    other = trade(pick(mine, core ^ 1, 0), "c", 1)
    parts = []
    for k in range(mine.shape[1]):
        part = jnp.stack([pick(own, column ^ k, 0), pick(other, column ^ k, 0)])
        parts.append(trade(part, "z", k) if k else part)
    return parts, other


def ffn_slices(sizes):
    core, column = lax.axis_index("c"), lax.axis_index("z")
    spots = [
        other * sizes["z"] + (column ^ k) for k in range(sizes["z"]) for other in (core, core ^ 1)
    ]
    return jnp.stack(spots).astype(jnp.int32)


def scatter_plane(partial):
    return total(list(all_to_all(partial, PLANE)))


def gather(block, axes):
    copies = jnp.broadcast_to(block, (lax.axis_size(axes),) + block.shape)
    return all_to_all(copies, axes)


VMEM_BYTES = 56 * 1024 * 1024
TILE = 256
NT = (((1,), (1,)), ((), ()))


def mm(left, right):
    return jnp.dot(left, right, preferred_element_type=F32)


def mm_nt(left, right):
    return lax.dot_general(left, right, NT, preferred_element_type=F32)


def causal(scores, start, tile):
    keys = lax.broadcasted_iota(jnp.int32, (tile, tile), 0)
    queries = lax.broadcasted_iota(jnp.int32, (tile, tile), 1)
    last = jnp.where(keys <= queries, scores[start:], -1e30)
    return last if start == 0 else jnp.concatenate([scores[:start], last], axis=0)


def forward_kernel(q_cols, kv_cols, seq, result, logsums):
    length = seq.shape[0]
    tile = min(TILE, length)
    per_kv = q_cols // kv_cols
    for e in range(kv_cols // HEAD_DIM):
        at = q_cols + e * HEAD_DIM
        keys = seq[:, at : at + HEAD_DIM]
        at = q_cols + kv_cols + e * HEAD_DIM
        values_t = seq[:, at : at + HEAD_DIM].T
        for start in range(0, length, tile):
            end = start + tile
            turned = []
            for h in range(e * per_kv, (e + 1) * per_kv):
                queries = seq[start:end, h * HEAD_DIM : (h + 1) * HEAD_DIM]
                scores = causal(mm_nt(keys[:end], queries) * HEAD_DIM ** (-0.5), start, tile)
                peak = jnp.max(scores, axis=0, keepdims=True)
                expd = jnp.exp(scores - peak)
                sums = jnp.sum(expd, axis=0, keepdims=True)
                logsums[h : h + 1, start:end] = peak + jnp.log(sums)
                probs = (expd * (1.0 / sums)).astype(BF)
                turned.append(mm(values_t[:, :end], probs))
            at = e * per_kv * HEAD_DIM
            result[start:end, at : at + per_kv * HEAD_DIM] = (
                jnp.concatenate(turned, axis=0).T.astype(BF)
            )


def backward_kernel(q_cols, kv_cols, seq, grads, logsums, result, key_sum, value_sum):
    length = seq.shape[0]
    tile = min(TILE, length)
    per_kv = q_cols // kv_cols
    scale = HEAD_DIM ** (-0.5)
    for e in range(kv_cols // HEAD_DIM):
        key_at = q_cols + e * HEAD_DIM
        value_at = q_cols + kv_cols + e * HEAD_DIM
        keys = seq[:, key_at : key_at + HEAD_DIM]
        keys_t = keys.T
        values = seq[:, value_at : value_at + HEAD_DIM]
        key_sum[...] = jnp.zeros_like(key_sum)
        value_sum[...] = jnp.zeros_like(value_sum)
        for start in range(0, length, tile):
            end = start + tile
            turned = []
            for h in range(e * per_kv, (e + 1) * per_kv):
                at = h * HEAD_DIM
                queries = seq[start:end, at : at + HEAD_DIM]
                grad = grads[start:end, at : at + HEAD_DIM]
                scores = causal(mm_nt(keys[:end], queries) * scale, start, tile)
                probs = jnp.exp(scores - logsums[h : h + 1, start:end])
                grad_probs = mm_nt(values[:end], grad)
                centred = jnp.sum(probs * grad_probs, axis=0, keepdims=True)
                grad_scores = (probs * (grad_probs - centred)).astype(BF)
                value_sum[:end, :] += mm(probs.astype(BF), grad)
                key_sum[:end, :] += mm(grad_scores, queries)
                turned.append(mm(keys_t[:, :end], grad_scores))
            at = e * per_kv * HEAD_DIM
            result[start:end, at : at + per_kv * HEAD_DIM] = (
                jnp.concatenate(turned, axis=0).T * scale
            ).astype(BF)
        result[:, key_at : key_at + HEAD_DIM] = (key_sum[...] * scale).astype(BF)
        result[:, value_at : value_at + HEAD_DIM] = value_sum[...].astype(BF)


def turn(values, cosine, sine, rotated):
    lane = lax.broadcasted_iota(jnp.int32, cosine.shape, 1)
    first_half = lane % HEAD_DIM < HEAD_DIM // 2
    parts = []
    for tile in range(values.shape[1] // 128):
        part = values[:, tile * 128 : (tile + 1) * 128]
        low, high = rotated[2 * tile], rotated[2 * tile + 1]
        if low or high:
            left = pltpu.roll(part, 128 - HEAD_DIM // 2, 1)
            right = pltpu.roll(part, HEAD_DIM // 2, 1)
            moved = part * cosine + jnp.where(first_half, left, right) * sine
            if low and high:
                part = moved
            else:
                part = jnp.where((lane < HEAD_DIM) == low, moved, part)
        parts.append(part)
    return jnp.concatenate(parts, axis=1)


def qkv_kernel(halves, rotated, x_ref, w_ref, cosine, sine, out_ref):
    piece, part = out_ref.shape[1:]
    for y in range(out_ref.shape[0] // halves):
        rows = pl.ds(y * piece, piece)
        values = mm(x_ref[rows, : w_ref.shape[0]], w_ref[...])
        values = turn(values, cosine[rows, :], sine[rows, :], rotated).astype(BF)
        for h in range(halves):
            out_ref[y * halves + h] = values[:, h * part : (h + 1) * part]


def heads_kernel(halves, x_ref, w_ref, out_ref):
    piece, cols = out_ref.shape[1:]
    for y in range(out_ref.shape[0] // halves):
        values = mm(x_ref[pl.ds(y * piece, piece), :], w_ref[...]).astype(BF)
        for h in range(halves):
            out_ref[y * halves + h] = values[:, h * cols : (h + 1) * cols]


def summed(parts):
    result = parts[0].astype(F32)
    for i in range(1, parts.shape[0]):
        result = result + parts[i].astype(F32)
    return result


def hidden_norm_kernel(parts, states, hidden_ref, unit_ref, factor_ref, copies):
    hidden = states[...] + summed(parts)
    unit, factor = norm_of(hidden)
    hidden_ref[...] = hidden
    unit_ref[...] = unit
    factor_ref[...] = factor
    for i in range(copies.shape[0]):
        copies[i] = unit.astype(BF)


def norm_back_kernel(parts, grad_out, unit, factor, grad_ref, copies):
    back = norm_backward(summed(parts), unit[...], factor[...])
    grad = grad_out[...].astype(F32) + back
    grad_ref[...] = grad
    for i in range(copies.shape[0]):
        copies[i] = grad.astype(BF)


def qkv_back_kernel(halves, rotated, blocks, w_ref, cosine, sine, grad_ref, out_ref):
    count, piece = blocks.shape[:2]
    for y in range(count // halves):
        rows = pl.ds(y * piece, piece)
        values = jnp.concatenate([blocks[y * halves + h] for h in range(halves)], axis=1)
        values = turn(values.astype(F32), cosine[rows, :], -sine[rows, :], rotated).astype(BF)
        grad_ref[rows, :] = values
        part = mm_nt(values, w_ref[...]).astype(BF)
        for x in range(piece // out_ref.shape[1]):
            out_ref[y * (piece // out_ref.shape[1]) + x] = part[
                x * out_ref.shape[1] : (x + 1) * out_ref.shape[1]
            ]


def o_kernel(halves, blocks, w_ref, tokens_ref, out_ref):
    count, piece = blocks.shape[:2]
    for y in range(count // halves):
        rows = pl.ds(y * piece, piece)
        values = jnp.concatenate([blocks[y * halves + h] for h in range(halves)], axis=1)
        tokens_ref[rows, :] = values
        part = mm_nt(values, w_ref[...]).astype(BF)
        for x in range(piece // out_ref.shape[1]):
            out_ref[y * (piece // out_ref.shape[1]) + x] = part[
                x * out_ref.shape[1] : (x + 1) * out_ref.shape[1]
            ]


def ffn_kernel(tiles, *refs):
    x_ref, dy_ref, gate_ref, up_ref, down_ref, gate_rows, up_rows = refs[:7]
    z_ref, dgate_ref, dup_ref, dx_ref, held_gate, held_up = refs[7:]
    step = pl.program_id(0)
    tile = gate_ref.shape[1]
    for i in range(tiles):

        @pl.when(step == i)
        def _():
            gate = mm(x_ref[...], gate_ref[...])
            up = mm(x_ref[...], up_ref[...])
            dz = mm(dy_ref[...], down_ref[...])
            sigmoid = jax.nn.sigmoid(gate)
            silu = gate * sigmoid
            z_ref[...] = (silu * up).astype(BF)
            dgate = (dz * up * sigmoid * (1.0 + gate * (1.0 - sigmoid))).astype(BF)
            dup = (dz * silu).astype(BF)
            dgate_ref[...] = dgate
            dup_ref[...] = dup
            held_gate[:, i * tile : (i + 1) * tile] = dgate
            held_up[:, i * tile : (i + 1) * tile] = dup

    @pl.when(step >= tiles)
    def _():
        part = mm_nt(held_gate[...], gate_rows[...]) + mm_nt(held_up[...], up_rows[...])
        dx_ref[...] = part.astype(dx_ref.dtype)


def ffn(tokens, grads, weights, out_dtype, ties=()):
    count, width = tokens.shape
    units = weights.shape[1] // 3
    tile, row_tile = min(256, units), min(1024, width)
    tiles, row_tiles = units // tile, width // row_tile

    def first(i):
        return jnp.minimum(i, tiles - 1)

    def second(i):
        return jnp.maximum(i - tiles, 0)

    whole = pl.BlockSpec((count, width), lambda i: (0, 0))
    narrow = pl.BlockSpec((count, tile), lambda i: (0, first(i)))
    columns = [
        pl.BlockSpec((width, tile), lambda i, j=j: (0, j * tiles + first(i))) for j in range(3)
    ]
    across = [pl.BlockSpec((row_tile, units), lambda i, j=j: (second(i), j)) for j in range(2)]
    hidden = jax.ShapeDtypeStruct((count, units), BF)
    return pl.pallas_call(
        skipping(functools.partial(ffn_kernel, tiles), 7, len(ties)),
        grid=(tiles + row_tiles,),
        out_shape=[hidden] * 3 + [jax.ShapeDtypeStruct((count, width), out_dtype)],
        in_specs=[whole, whole]
        + columns
        + across
        + [pl.BlockSpec(memory_space=pl.ANY)] * len(ties),
        out_specs=[narrow] * 3 + [pl.BlockSpec((count, row_tile), lambda i: (0, second(i)))],
        scratch_shapes=[pltpu.VMEM((count, units), BF)] * 2,
        compiler_params=pltpu.CompilerParams(vmem_limit_bytes=VMEM_BYTES),
        cost_estimate=pl.CostEstimate(
            flops=10 * count * width * units,
            bytes_accessed=10 * width * units,
            transcendentals=count * units,
        ),
    )(tokens, grads, *[weights] * 5, *ties)


def add_product_kernel(z_ref, down_ref, *refs):
    part = mm_nt(z_ref[...], down_ref[...])
    for held in refs[:-1]:
        part = part + held[...].astype(F32)
    refs[-1][...] = part.astype(BF)


def add_product(z, weights, *added):
    count, units = z.shape
    width = weights.shape[0]
    tile = min(512, width)
    part = pl.BlockSpec((count, tile), lambda i: (0, i))
    return pl.pallas_call(
        add_product_kernel,
        grid=(width // tile,),
        out_shape=jax.ShapeDtypeStruct((count, width), BF),
        in_specs=[
            pl.BlockSpec((count, units), lambda i: (0, 0)),
            pl.BlockSpec((tile, units), lambda i: (i, 2)),
        ]
        + [part] * len(added),
        out_specs=part,
        compiler_params=pltpu.CompilerParams(vmem_limit_bytes=VMEM_BYTES),
        cost_estimate=pl.CostEstimate(flops=1, bytes_accessed=1, transcendentals=0),
    )(z, weights, *added)


def outer_kernel(*refs):
    tokens, grads = refs[0:2], refs[2:4]
    dgate, dup, hidden, out_ref = refs[4:6], refs[6:8], refs[8:10], refs[10]
    units = hidden[0].shape[1]
    tokens_t = [half[...].T for half in tokens]
    grads_t = [half[...].T for half in grads]
    for j, (left, right) in enumerate(((tokens_t, dgate), (tokens_t, dup), (grads_t, hidden))):
        part = mm(left[0], right[0][...]) + mm(left[1], right[1][...])
        out_ref[:, j * units : (j + 1) * units] = part.astype(BF)


def outer(tokens, grads, dgate, dup, hidden):
    count, width = tokens[0].shape
    units = hidden[0].shape[1]
    tile = min(512, width)
    narrow = pl.BlockSpec((count, tile), lambda i: (0, i))
    whole = pl.BlockSpec((count, units), lambda i: (0, 0))
    return pl.pallas_call(
        outer_kernel,
        grid=(width // tile,),
        out_shape=jax.ShapeDtypeStruct((width, 3 * units), BF),
        in_specs=[narrow] * 4 + [whole] * 6,
        out_specs=pl.BlockSpec((tile, 3 * units), lambda i: (i, 0)),
        compiler_params=pltpu.CompilerParams(vmem_limit_bytes=VMEM_BYTES),
        cost_estimate=pl.CostEstimate(flops=1, bytes_accessed=1, transcendentals=0),
    )(*tokens, *grads, *dgate, *dup, *hidden)


def finish_kernel(slices, *refs):
    pieces = len(refs) - 8
    spots, parts = refs[0], refs[1 : 1 + pieces]
    weights, gain = refs[1 + pieces : 3 + pieces], refs[3 + pieces]
    outs, gain_out = refs[4 + pieces : 7 + pieces], refs[7 + pieces]
    width = outs[0].shape[1] // slices
    found = 0.0
    for k in range(pieces):
        for i in range(parts[k].shape[0]):
            spot = spots[k * parts[k].shape[0] + i]
            columns = pl.ds(pl.multiple_of(spot * width, width), width)
            for j in range(2):
                part = parts[k][i, :, j * width : (j + 1) * width].astype(F32)
                outs[j][:, columns] = part * gain[...]
                found = found + part * weights[j][:, columns].astype(F32)
            outs[2][:, columns] = parts[k][i, :, 2 * width :].astype(F32)
    gain_out[...] = jnp.sum(found, axis=1, keepdims=True)


def finish(parts, spots, weights, gain):
    rows = gain.shape[0]
    return in_vmem(
        functools.partial(finish_kernel, sum(part.shape[0] for part in parts)),
        list(parts) + list(weights) + [gain],
        [jax.ShapeDtypeStruct(weights[0].shape, F32)] * 3 + [jax.ShapeDtypeStruct((rows, 1), F32)],
        [],
        spots,
    )


def skipping(kernel, at, count):
    return lambda *refs: kernel(*refs[:at], *refs[at + count :])


def in_vmem(kernel, operands, outs, scratch, places=None, ties=()):
    first = [] if places is None else [places]
    kernel = skipping(kernel, len(first) + len(operands), len(ties))
    return pl.pallas_call(
        kernel,
        out_shape=outs,
        in_specs=[pl.BlockSpec(memory_space=pltpu.SMEM)] * len(first)
        + kernel_specs(len(operands))
        + [pl.BlockSpec(memory_space=pl.ANY)] * len(ties),
        out_specs=kernel_specs(len(outs)),
        scratch_shapes=scratch,
        compiler_params=pltpu.CompilerParams(vmem_limit_bytes=VMEM_BYTES),
        cost_estimate=pl.CostEstimate(flops=1, bytes_accessed=1, transcendentals=0),
    )(*first, *operands, *ties)


def kernel_specs(count):
    return [pl.BlockSpec(memory_space=pltpu.VMEM)] * count


def attention_forward(seq, q_cols, kv_cols, ties):
    length = seq.shape[0]
    return in_vmem(
        functools.partial(forward_kernel, q_cols, kv_cols),
        [seq],
        [
            jax.ShapeDtypeStruct((length, q_cols), BF),
            jax.ShapeDtypeStruct((q_cols // HEAD_DIM, length), F32),
        ],
        [],
        ties=ties,
    )


def attention_backward(seq, grads, logsums, q_cols, kv_cols):
    length = seq.shape[0]
    return in_vmem(
        functools.partial(backward_kernel, q_cols, kv_cols),
        [seq, grads, logsums],
        [jax.ShapeDtypeStruct(seq.shape, BF)],
        [pltpu.VMEM((length, HEAD_DIM), F32)] * 2,
    )[0]


def body(
    inputs,
    positions,
    attn_gain,
    q_weight,
    k_weight,
    v_weight,
    o_weight,
    ffn_gain,
    gate_weight,
    up_weight,
    down_weight,
    cotangent,
):
    sizes = {axis: lax.axis_size(axis) for axis in "yczx"}
    yn, cn, zn, xn = [sizes[axis] for axis in "yczx"]
    _, span, width = inputs.shape
    slices = yn * xn
    expanded = max(KV_HEADS, 2 * slices)
    copies = expanded // KV_HEADS
    rows = q_weight.shape[0]
    halves = zn // yn
    q_cols = HEADS * HEAD_DIM // (slices * halves)
    kv_cols = expanded * HEAD_DIM // (slices * halves)
    part_cols = q_cols + 2 * kv_cols
    piece = xn * span
    length = zn * piece

    states = reorder(inputs.reshape(span, width), sizes, "yczx", F32)
    grad_low = reorder(cotangent.reshape(span, width), sizes, "yczx", BF)

    gain_one = attn_gain.astype(F32)[:, None]
    gain_two = ffn_gain.astype(F32)[:, None]

    def widen(weight):
        return jnp.repeat(weight.reshape(rows, KV_HEADS, HEAD_DIM), copies, axis=1)

    def parts(weight, cols):
        return weight.reshape(rows, slices, halves, cols)

    wide_k, wide_v = widen(k_weight), widen(v_weight)
    qkv_rows = (
        jnp.concatenate(
            [parts(q_weight, q_cols), parts(wide_k, kv_cols), parts(wide_v, kv_cols)], axis=3
        )
        .reshape(rows, slices, halves * part_cols)
        .transpose(1, 0, 2)
    )
    qkv_scaled = (qkv_rows.astype(F32) * gain_one[None]).astype(BF)
    gate_scaled = (gate_weight.astype(F32) * gain_two).astype(BF)
    up_scaled = (up_weight.astype(F32) * gain_two).astype(BF)

    unit_one, factor_one = norm_of(states)
    o_rows = o_weight.reshape(rows, slices, halves * q_cols).transpose(1, 0, 2)
    near_attn = in_order(swap(jnp.concatenate([qkv_scaled, o_rows], axis=2), PLANE), PLANE)
    ffn_near = ffn_weights_near((gate_scaled, up_scaled, down_weight), sizes)
    digits = jnp.stack([positions.reshape(span) // 128, positions.reshape(span) % 128], axis=1)
    digits = jnp.repeat(digits.astype(BF), HEAD_DIM, axis=1)
    tokens_one = lax.all_gather(
        jnp.concatenate([unit_one.astype(BF), digits], axis=1), PLANE, axis=0, tiled=True
    )
    ffn_full = ffn_weights_far(after(ffn_near, near_attn))
    qkv_width = halves * part_cols
    qkv_own = spread(after(near_attn[..., :qkv_width], ffn_near), "z")
    o_own = spread(after(near_attn[..., qkv_width:], *qkv_own[1:]), "z")
    qkv_full = attention_weights(qkv_own, sizes)
    digits = tokens_one[:, width:].astype(F32)
    cosine, sine = angles_of(digits[:, 0] * 128.0 + digits[:, HEAD_DIM])
    cosine = jnp.concatenate([cosine] * 4, axis=1)
    sine = jnp.concatenate([-sine, sine] * 2, axis=1)
    rotated = ([True] * ((q_cols + kv_cols) // HEAD_DIM) + [False] * (kv_cols // HEAD_DIM)) * halves
    count = slices * span

    (packed,) = in_vmem(
        functools.partial(qkv_kernel, halves, rotated),
        [tokens_one, qkv_full, cosine, sine],
        [jax.ShapeDtypeStruct((zn, piece, part_cols), BF)],
        [],
    )
    heads_in = all_to_all(packed, "z").reshape(length, part_cols)
    attended, logsums = attention_forward(heads_in, q_cols, kv_cols, o_own[1:])
    o_full = attention_weights(o_own, sizes)
    grad_near = lax.all_gather(after(grad_low, attended), "z", axis=0, tiled=False)
    attended = all_to_all(attended.reshape(zn, piece, q_cols), "z")

    attn_tokens, o_part = in_vmem(
        functools.partial(o_kernel, halves),
        [attended, o_full],
        [
            jax.ShapeDtypeStruct((count, halves * q_cols), BF),
            jax.ShapeDtypeStruct((slices, span, width), BF),
        ],
        [],
    )
    square = jax.ShapeDtypeStruct((span, width), F32)
    hidden_one, unit_two, factor_two, tokens_near = in_vmem(
        hidden_norm_kernel,
        [all_to_all(o_part, PLANE), states],
        [
            square,
            square,
            jax.ShapeDtypeStruct((span, 1), F32),
            jax.ShapeDtypeStruct((zn, span, width), BF),
        ],
        [],
        ties=[ffn_full],
    )

    grad_far = trade(grad_near, "c", 1)
    tokens_near = all_to_all(tokens_near, "z")
    tokens_far = trade(tokens_near, "c", 1)
    tokens_near, tokens_far, grad_near, grad_far = [
        array.reshape(-1, width) for array in (tokens_near, tokens_far, grad_near, grad_far)
    ]
    z_far, dgate_far, dup_far, dx_far = ffn(tokens_far, grad_far, ffn_full, BF)
    z_near, dgate_near, dup_near, dx_near = ffn(
        tokens_near, grad_near, ffn_full, F32, [dx_far]
    )
    blocks = (zn, span, width)
    grad_both = dx_near.reshape(blocks) + trade(dx_far.reshape(blocks), "c", 1).astype(F32)
    grad_both = grad_both.astype(BF)
    grad_there = all_to_all(grad_both, "z")
    ffn_part = outer(
        (tokens_near, tokens_far),
        (grad_near, grad_far),
        (dgate_near, dgate_far),
        (dup_near, dup_far),
        (z_near, z_far),
    )
    result_far = add_product(z_far, ffn_full)
    result_near = add_product(z_near, ffn_full, trade(result_far, "c", 1)).reshape(blocks)
    grad_one, branch_tokens = in_vmem(
        norm_back_kernel,
        [grad_there, grad_low, unit_two, factor_two],
        [square, jax.ShapeDtypeStruct((slices, span, width), BF)],
        [],
        ties=[result_near, ffn_part],
    )
    result_there = swap(result_near, "z")

    branch_tokens = all_to_all(branch_tokens, PLANE).reshape(-1, width)
    (grad_attn,) = in_vmem(
        functools.partial(heads_kernel, halves),
        [branch_tokens, o_full],
        [jax.ShapeDtypeStruct((zn, piece, q_cols), BF)],
        [],
        ties=result_there[1:3],
    )
    ffn_sum = ffn_grads(after(ffn_part, grad_attn), sizes)
    grad_heads = all_to_all(grad_attn, "z")
    grad_heads = grad_heads.reshape(length, q_cols)
    heads_out = attention_backward(heads_in, grad_heads, logsums, q_cols, kv_cols)
    back = all_to_all(heads_out.reshape(zn, piece, part_cols), "z")
    ffn_sum, _ = ffn_grads_near(ffn_sum)
    output = (after(hidden_one, grad_heads) + total(result_there)).astype(BF)
    grad_qkv, hat_part = in_vmem(
        functools.partial(qkv_back_kernel, halves, rotated),
        [back, qkv_full, cosine, sine],
        [
            jax.ShapeDtypeStruct((count, halves * part_cols), BF),
            jax.ShapeDtypeStruct((slices, span, width), BF),
        ],
        [],
    )
    grad_hat_one = after(scatter_plane(hat_part), result_there[3])
    input_grad = grad_one + norm_backward(grad_hat_one, unit_one, factor_one)
    qkv_part = contract_rows(tokens_one[:, :width], grad_qkv)
    qkv_sum, qkv_there = attention_grads(qkv_part, sizes, [], [])
    o_sum, _ = attention_grads(contract_rows(branch_tokens, attn_tokens), sizes, qkv_there, [])
    attn_gain_grad = jnp.sum(qkv_sum * qkv_rows.astype(F32), axis=(0, 2))
    qkv_grad = (qkv_sum * gain_one[None]).transpose(1, 0, 2)
    qkv_grad = qkv_grad.reshape(rows, slices, halves, part_cols)
    spots = ffn_slices(sizes)
    gate_grad, up_grad, down_grad, ffn_gain_grad = finish(
        ffn_sum, spots, (gate_weight, up_weight), gain_two
    )

    def narrow(part):
        part = part.reshape(rows, KV_HEADS, copies, HEAD_DIM).sum(axis=2)
        return part.reshape(rows, KV_HEADS * HEAD_DIM)

    q_grad = qkv_grad[..., :q_cols].reshape(rows, HEADS * HEAD_DIM)
    k_grad = narrow(qkv_grad[..., q_cols : q_cols + kv_cols])
    v_grad = narrow(qkv_grad[..., q_cols + kv_cols :])
    return (
        reorder(output, sizes, "yxcz", BF).reshape(1, span, width),
        reorder(input_grad, sizes, "yxcz", F32).reshape(1, span, width),
        attn_gain_grad,
        q_grad,
        k_grad,
        v_grad,
        o_sum.transpose(1, 0, 2).reshape(rows, HEADS * HEAD_DIM),
        ffn_gain_grad.reshape(rows),
        gate_grad,
        up_grad,
        down_grad,
    )


def solution(mesh):
    batch, seq = mesh.devices.shape
    cores, column = 2, 4
    parts = mesh.devices.reshape(batch // cores, cores, column, seq // column)
    tokens = P(("y", "c"), ("z", "x"), None)
    rows = P(("y", "c", "z", "x"), None)
    gain = P(("y", "c", "z", "x"))
    return jax.shard_map(
        body,
        mesh=Mesh(parts, ("y", "c", "z", "x")),
        in_specs=(
            tokens, P(("y", "c"), ("z", "x")), gain, rows, rows, rows, rows, gain, rows, rows, rows,
            tokens,
        ),
        out_specs=(tokens, tokens, gain, rows, rows, rows, rows, gain, rows, rows, rows),
        check_vma=False,
    )
```

```python
import functools
import math

import jax
import jax.numpy as jnp
import numpy as np
from jax import lax
from jax.experimental import pallas as pl
from jax.experimental.pallas import tpu as pltpu
from jax.sharding import Mesh, PartitionSpec as P

HEADS = 32
KV_HEADS = 8
HEAD_DIM = 64

epsilon = 1e-05
rope_base = 500000.0
rope_scale = 32.0
low_freq = 1.0
high_freq = 4.0
initial_context = 8192.0

BF = jnp.bfloat16
F32 = jnp.float32


def frequencies():
    half = HEAD_DIM // 2
    base_freqs = rope_base ** (-(jnp.arange(half, dtype=F32) * 2.0 / HEAD_DIM))
    wavelen = 2.0 * math.pi / base_freqs
    smooth = (initial_context / wavelen - low_freq) / (high_freq - low_freq)
    middle = (1.0 - smooth) * base_freqs / rope_scale + smooth * base_freqs
    return jnp.where(
        wavelen < initial_context / high_freq,
        base_freqs,
        jnp.where(wavelen > initial_context / low_freq, base_freqs / rope_scale, middle),
    )


def angles_of(positions):
    turned = positions.astype(F32)[:, None] * frequencies()[None, :]
    return (jnp.cos(turned), jnp.sin(turned))


def contract_rows(left, right):
    return jnp.einsum("ra,rb->ab", left, right, preferred_element_type=F32)


def product_t(left, right):
    return jnp.einsum("rc,dc->rd", left, right, preferred_element_type=F32)


def product(left, right):
    return jnp.dot(left, right, preferred_element_type=F32)


def norm_of(values):
    factor = lax.rsqrt(jnp.mean(values * values, axis=-1, keepdims=True) + epsilon)
    return (values * factor, factor)


def norm_backward(grad_hat, normed, factor):
    return factor * (grad_hat - normed * jnp.mean(grad_hat * normed, axis=-1, keepdims=True))


def pick(array, index, axis):
    return lax.dynamic_index_in_dim(array, index, axis, keepdims=False)


def put(buffer, block, *places):
    shape, start = list(buffer.shape), [0] * buffer.ndim
    for axis, index in places:
        shape[axis], start[axis] = 1, index
    return lax.dynamic_update_slice(buffer, block.reshape(shape), start)


def after(value, *others):
    zero = jnp.zeros((), value.dtype)
    for array in others:
        first = array[(0,) * array.ndim]
        zero = zero + (first != first).astype(value.dtype)
    corner = value[tuple(slice(0, min(n, 16 if i < value.ndim - 1 else 128)) if i >= value.ndim - 2
                         else slice(0, 1) for i, n in enumerate(value.shape))]
    return lax.dynamic_update_slice(value, corner + zero, (0,) * value.ndim)


PLANE = ("y", "x")
COLUMN = ("c", "z")


def place(axes):
    return lax.axis_index(axes), lax.axis_size(axes)


def trade(value, axes, step):
    count = lax.axis_size(axes)
    return lax.ppermute(value, axes, [(i, i ^ step) for i in range(count)])


def swap(blocks, axes, at=0):
    here, count = place(axes)
    return [pick(blocks, here, at)] + [
        trade(pick(blocks, here ^ k, at), axes, k) for k in range(1, count)
    ]


def spread(block, axes):
    count = lax.axis_size(axes)
    return [block] + [trade(block, axes, k) for k in range(1, count)]


def in_order(blocks, axes):
    here, count = place(axes)
    out = jnp.zeros((count,) + blocks[0].shape, blocks[0].dtype)
    for k, block in enumerate(blocks):
        out = put(out, block, (0, here ^ k))
    return out


def total(blocks):
    result = blocks[0].astype(F32)
    for block in blocks[1:]:
        result = result + block.astype(F32)
    return result


def order_kernel(order, group, in_ref, out_ref):
    wide = max(group, 128)
    for at in range(0, out_ref.shape[1], wide):
        first = at // group
        parts = [
            in_ref[:, j * group : (j + 1) * group] for j in order[first : first + wide // group]
        ]
        out_ref[:, at : at + wide] = jnp.concatenate(parts, axis=1).astype(out_ref.dtype)


def reorder(features, sizes, before, dtype):
    later = "yxcz" if before == "yczx" else "yczx"
    count = math.prod(sizes.values())
    axes = np.arange(count).reshape([sizes[axis] for axis in before])
    order = axes.transpose([before.index(axis) for axis in later]).reshape(-1).tolist()
    return in_vmem(
        functools.partial(order_kernel, order, features.shape[1] // count),
        [features],
        [jax.ShapeDtypeStruct(features.shape, dtype)],
        [],
    )[0]


def attention_weights(own, sizes):
    yn, cn, zn, xn = [sizes[axis] for axis in "yczx"]
    rows, cols = own[0].shape[1:]
    core, column = lax.axis_index("c"), lax.axis_index("z")
    full = jnp.zeros((yn * xn, cn, zn, rows, cols), BF)
    for k in range(zn):
        full = put(full, own[k], (1, core), (2, column ^ k))
    other = trade(pick(full, core, 1), "c", 1)
    return put(full, other, (1, core ^ 1)).reshape(-1, cols)


def attention_grads(partial, sizes, earlier, later):
    yn, cn, zn, xn = [sizes[axis] for axis in "yczx"]
    cols = partial.shape[-1]
    blocks = partial.reshape(yn * xn, cn, zn, -1, cols)
    core = lax.axis_index("c")
    got = trade(pick(blocks, core ^ 1, 1).astype(BF), "c", 1)
    near = (pick(blocks, core, 1) + got.astype(F32)).astype(BF)
    near = after(near, *earlier)
    there = swap(near, "z", 1)
    mine = after(total(there).astype(BF), *later)
    return in_order(swap(mine, PLANE), PLANE).astype(F32), there[1:], near


def all_to_all(blocks, axes):
    return lax.all_to_all(blocks, axes, split_axis=0, concat_axis=0, tiled=True)


def ffn_weights_near(weights, sizes):
    slices = sizes["c"] * sizes["z"]
    split = [w.reshape(w.shape[0], slices, -1).transpose(1, 0, 2) for w in weights]
    return all_to_all(jnp.concatenate(split, axis=2), COLUMN)


def ffn_weights_far(near):
    full = lax.all_gather(near, PLANE, axis=0, tiled=False)
    return full.reshape(-1, near.shape[-1])


def ffn_grads(partial, sizes):
    cols = partial.shape[-1]
    blocks = partial.reshape(sizes["y"] * sizes["x"], -1, cols)
    mine = lax.psum_scatter(blocks, PLANE, scatter_dimension=0, tiled=False)
    return mine.reshape(sizes["c"], sizes["z"], -1, cols)


def ffn_grads_near(mine):
    core, column = lax.axis_index("c"), lax.axis_index("z")
    own = pick(mine, core, 0)
    other = trade(pick(mine, core ^ 1, 0), "c", 1)
    parts = []
    for k in range(mine.shape[1]):
        part = jnp.stack([pick(own, column ^ k, 0), pick(other, column ^ k, 0)])
        parts.append(trade(part, "z", k) if k else part)
    return parts, other


def ffn_slices(sizes):
    core, column = lax.axis_index("c"), lax.axis_index("z")
    spots = [
        other * sizes["z"] + (column ^ k) for k in range(sizes["z"]) for other in (core, core ^ 1)
    ]
    return jnp.stack(spots).astype(jnp.int32)


def scatter_plane(partial):
    return total(list(all_to_all(partial, PLANE)))


def gather(block, axes):
    copies = jnp.broadcast_to(block, (lax.axis_size(axes),) + block.shape)
    return all_to_all(copies, axes)


VMEM_BYTES = 56 * 1024 * 1024
TILE = 256
NT = (((1,), (1,)), ((), ()))


def mm(left, right):
    return jnp.dot(left, right, preferred_element_type=F32)


def mm_nt(left, right):
    return lax.dot_general(left, right, NT, preferred_element_type=F32)


def causal(scores, start, tile):
    keys = lax.broadcasted_iota(jnp.int32, (tile, tile), 0)
    queries = lax.broadcasted_iota(jnp.int32, (tile, tile), 1)
    last = jnp.where(keys <= queries, scores[start:], -1e30)
    return last if start == 0 else jnp.concatenate([scores[:start], last], axis=0)


def forward_kernel(q_cols, kv_cols, seq, result, logsums):
    length = seq.shape[0]
    tile = min(TILE, length)
    per_kv = q_cols // kv_cols
    for e in range(kv_cols // HEAD_DIM):
        at = q_cols + e * HEAD_DIM
        keys = seq[:, at : at + HEAD_DIM]
        at = q_cols + kv_cols + e * HEAD_DIM
        values_t = seq[:, at : at + HEAD_DIM].T
        for start in range(0, length, tile):
            end = start + tile
            turned = []
            for h in range(e * per_kv, (e + 1) * per_kv):
                queries = seq[start:end, h * HEAD_DIM : (h + 1) * HEAD_DIM]
                scores = causal(mm_nt(keys[:end], queries) * HEAD_DIM ** (-0.5), start, tile)
                peak = jnp.max(scores, axis=0, keepdims=True)
                expd = jnp.exp(scores - peak)
                sums = jnp.sum(expd, axis=0, keepdims=True)
                logsums[h : h + 1, start:end] = peak + jnp.log(sums)
                probs = (expd * (1.0 / sums)).astype(BF)
                turned.append(mm(values_t[:, :end], probs))
            at = e * per_kv * HEAD_DIM
            result[start:end, at : at + per_kv * HEAD_DIM] = (
                jnp.concatenate(turned, axis=0).T.astype(BF)
            )


def backward_kernel(q_cols, kv_cols, seq, grads, logsums, result, key_sum, value_sum):
    length = seq.shape[0]
    tile = min(TILE, length)
    per_kv = q_cols // kv_cols
    scale = HEAD_DIM ** (-0.5)
    for e in range(kv_cols // HEAD_DIM):
        key_at = q_cols + e * HEAD_DIM
        value_at = q_cols + kv_cols + e * HEAD_DIM
        keys = seq[:, key_at : key_at + HEAD_DIM]
        keys_t = keys.T
        values = seq[:, value_at : value_at + HEAD_DIM]
        key_sum[...] = jnp.zeros_like(key_sum)
        value_sum[...] = jnp.zeros_like(value_sum)
        for start in range(0, length, tile):
            end = start + tile
            turned = []
            for h in range(e * per_kv, (e + 1) * per_kv):
                at = h * HEAD_DIM
                queries = seq[start:end, at : at + HEAD_DIM]
                grad = grads[start:end, at : at + HEAD_DIM]
                scores = causal(mm_nt(keys[:end], queries) * scale, start, tile)
                probs = jnp.exp(scores - logsums[h : h + 1, start:end])
                grad_probs = mm_nt(values[:end], grad)
                centred = jnp.sum(probs * grad_probs, axis=0, keepdims=True)
                grad_scores = (probs * (grad_probs - centred)).astype(BF)
                value_sum[:end, :] += mm(probs.astype(BF), grad)
                key_sum[:end, :] += mm(grad_scores, queries)
                turned.append(mm(keys_t[:, :end], grad_scores))
            at = e * per_kv * HEAD_DIM
            result[start:end, at : at + per_kv * HEAD_DIM] = (
                jnp.concatenate(turned, axis=0).T * scale
            ).astype(BF)
        result[:, key_at : key_at + HEAD_DIM] = (key_sum[...] * scale).astype(BF)
        result[:, value_at : value_at + HEAD_DIM] = value_sum[...].astype(BF)


def turn(values, cosine, sine, rotated):
    lane = lax.broadcasted_iota(jnp.int32, cosine.shape, 1)
    first_half = lane % HEAD_DIM < HEAD_DIM // 2
    parts = []
    for tile in range(values.shape[1] // 128):
        part = values[:, tile * 128 : (tile + 1) * 128]
        low, high = rotated[2 * tile], rotated[2 * tile + 1]
        if low or high:
            left = pltpu.roll(part, 128 - HEAD_DIM // 2, 1)
            right = pltpu.roll(part, HEAD_DIM // 2, 1)
            moved = part * cosine + jnp.where(first_half, left, right) * sine
            if low and high:
                part = moved
            else:
                part = jnp.where((lane < HEAD_DIM) == low, moved, part)
        parts.append(part)
    return jnp.concatenate(parts, axis=1)


def qkv_kernel(halves, rotated, x_ref, w_ref, cosine, sine, out_ref):
    piece, part = out_ref.shape[1:]
    for y in range(out_ref.shape[0] // halves):
        rows = pl.ds(y * piece, piece)
        values = mm(x_ref[rows, : w_ref.shape[0]], w_ref[...])
        values = turn(values, cosine[rows, :], sine[rows, :], rotated).astype(BF)
        for h in range(halves):
            out_ref[y * halves + h] = values[:, h * part : (h + 1) * part]


def heads_kernel(halves, x_ref, w_ref, out_ref):
    piece, cols = out_ref.shape[1:]
    for y in range(out_ref.shape[0] // halves):
        values = mm(x_ref[pl.ds(y * piece, piece), :], w_ref[...]).astype(BF)
        for h in range(halves):
            out_ref[y * halves + h] = values[:, h * cols : (h + 1) * cols]


def summed(parts):
    result = parts[0].astype(F32)
    for i in range(1, parts.shape[0]):
        result = result + parts[i].astype(F32)
    return result


def hidden_norm_kernel(parts, states, hidden_ref, unit_ref, factor_ref, copies):
    hidden = states[...] + summed(parts)
    unit, factor = norm_of(hidden)
    hidden_ref[...] = hidden
    unit_ref[...] = unit
    factor_ref[...] = factor
    for i in range(copies.shape[0]):
        copies[i] = unit.astype(BF)


def norm_back_kernel(parts, grad_out, unit, factor, grad_ref, copies):
    back = norm_backward(summed(parts), unit[...], factor[...])
    grad = grad_out[...].astype(F32) + back
    grad_ref[...] = grad
    for i in range(copies.shape[0]):
        copies[i] = grad.astype(BF)


def qkv_back_kernel(halves, rotated, blocks, w_ref, cosine, sine, grad_ref, out_ref):
    count, piece = blocks.shape[:2]
    for y in range(count // halves):
        rows = pl.ds(y * piece, piece)
        values = jnp.concatenate([blocks[y * halves + h] for h in range(halves)], axis=1)
        values = turn(values.astype(F32), cosine[rows, :], -sine[rows, :], rotated).astype(BF)
        grad_ref[rows, :] = values
        part = mm_nt(values, w_ref[...]).astype(BF)
        for x in range(piece // out_ref.shape[1]):
            out_ref[y * (piece // out_ref.shape[1]) + x] = part[
                x * out_ref.shape[1] : (x + 1) * out_ref.shape[1]
            ]


def o_kernel(halves, blocks, w_ref, tokens_ref, out_ref):
    count, piece = blocks.shape[:2]
    for y in range(count // halves):
        rows = pl.ds(y * piece, piece)
        values = jnp.concatenate([blocks[y * halves + h] for h in range(halves)], axis=1)
        tokens_ref[rows, :] = values
        part = mm_nt(values, w_ref[...]).astype(BF)
        for x in range(piece // out_ref.shape[1]):
            out_ref[y * (piece // out_ref.shape[1]) + x] = part[
                x * out_ref.shape[1] : (x + 1) * out_ref.shape[1]
            ]


def ffn_kernel(tiles, *refs):
    x_ref, dy_ref, gate_ref, up_ref, down_ref, gate_rows, up_rows = refs[:7]
    z_ref, dgate_ref, dup_ref, dx_ref, held_gate, held_up = refs[7:]
    step = pl.program_id(0)
    tile = gate_ref.shape[1]
    for i in range(tiles):

        @pl.when(step == i)
        def _():
            gate = mm(x_ref[...], gate_ref[...])
            up = mm(x_ref[...], up_ref[...])
            dz = mm(dy_ref[...], down_ref[...])
            sigmoid = jax.nn.sigmoid(gate)
            silu = gate * sigmoid
            z_ref[...] = (silu * up).astype(BF)
            dgate = (dz * up * sigmoid * (1.0 + gate * (1.0 - sigmoid))).astype(BF)
            dup = (dz * silu).astype(BF)
            dgate_ref[...] = dgate
            dup_ref[...] = dup
            held_gate[:, i * tile : (i + 1) * tile] = dgate
            held_up[:, i * tile : (i + 1) * tile] = dup

    @pl.when(step >= tiles)
    def _():
        part = mm_nt(held_gate[...], gate_rows[...]) + mm_nt(held_up[...], up_rows[...])
        dx_ref[...] = part.astype(dx_ref.dtype)


def ffn(tokens, grads, weights, out_dtype, ties=()):
    count, width = tokens.shape
    units = weights.shape[1] // 3
    tile, row_tile = min(256, units), min(1024, width)
    tiles, row_tiles = units // tile, width // row_tile

    def first(i):
        return jnp.minimum(i, tiles - 1)

    def second(i):
        return jnp.maximum(i - tiles, 0)

    whole = pl.BlockSpec((count, width), lambda i: (0, 0))
    narrow = pl.BlockSpec((count, tile), lambda i: (0, first(i)))
    columns = [
        pl.BlockSpec((width, tile), lambda i, j=j: (0, j * tiles + first(i))) for j in range(3)
    ]
    across = [pl.BlockSpec((row_tile, units), lambda i, j=j: (second(i), j)) for j in range(2)]
    hidden = jax.ShapeDtypeStruct((count, units), BF)
    return pl.pallas_call(
        skipping(functools.partial(ffn_kernel, tiles), 7, len(ties)),
        grid=(tiles + row_tiles,),
        out_shape=[hidden] * 3 + [jax.ShapeDtypeStruct((count, width), out_dtype)],
        in_specs=[whole, whole]
        + columns
        + across
        + [pl.BlockSpec(memory_space=pl.ANY)] * len(ties),
        out_specs=[narrow] * 3 + [pl.BlockSpec((count, row_tile), lambda i: (0, second(i)))],
        scratch_shapes=[pltpu.VMEM((count, units), BF)] * 2,
        compiler_params=pltpu.CompilerParams(vmem_limit_bytes=VMEM_BYTES),
        cost_estimate=pl.CostEstimate(
            flops=10 * count * width * units,
            bytes_accessed=10 * width * units,
            transcendentals=count * units,
        ),
    )(tokens, grads, *[weights] * 5, *ties)


def add_product_kernel(z_ref, down_ref, *refs):
    part = mm_nt(z_ref[...], down_ref[...])
    for held in refs[:-1]:
        part = part + held[...].astype(F32)
    refs[-1][...] = part.astype(BF)


def add_product(z, weights, *added):
    count, units = z.shape
    width = weights.shape[0]
    tile = min(512, width)
    part = pl.BlockSpec((count, tile), lambda i: (0, i))
    return pl.pallas_call(
        add_product_kernel,
        grid=(width // tile,),
        out_shape=jax.ShapeDtypeStruct((count, width), BF),
        in_specs=[
            pl.BlockSpec((count, units), lambda i: (0, 0)),
            pl.BlockSpec((tile, units), lambda i: (i, 2)),
        ]
        + [part] * len(added),
        out_specs=part,
        compiler_params=pltpu.CompilerParams(vmem_limit_bytes=VMEM_BYTES),
        cost_estimate=pl.CostEstimate(flops=1, bytes_accessed=1, transcendentals=0),
    )(z, weights, *added)


def outer_kernel(*refs):
    tokens, grads = refs[0:2], refs[2:4]
    dgate, dup, hidden, out_ref = refs[4:6], refs[6:8], refs[8:10], refs[10]
    units = hidden[0].shape[1]
    tokens_t = [half[...].T for half in tokens]
    grads_t = [half[...].T for half in grads]
    for j, (left, right) in enumerate(((tokens_t, dgate), (tokens_t, dup), (grads_t, hidden))):
        part = mm(left[0], right[0][...]) + mm(left[1], right[1][...])
        out_ref[:, j * units : (j + 1) * units] = part.astype(BF)


def outer(tokens, grads, dgate, dup, hidden):
    count, width = tokens[0].shape
    units = hidden[0].shape[1]
    tile = min(512, width)
    narrow = pl.BlockSpec((count, tile), lambda i: (0, i))
    whole = pl.BlockSpec((count, units), lambda i: (0, 0))
    return pl.pallas_call(
        outer_kernel,
        grid=(width // tile,),
        out_shape=jax.ShapeDtypeStruct((width, 3 * units), BF),
        in_specs=[narrow] * 4 + [whole] * 6,
        out_specs=pl.BlockSpec((tile, 3 * units), lambda i: (i, 0)),
        compiler_params=pltpu.CompilerParams(vmem_limit_bytes=VMEM_BYTES),
        cost_estimate=pl.CostEstimate(flops=1, bytes_accessed=1, transcendentals=0),
    )(*tokens, *grads, *dgate, *dup, *hidden)


def finish_kernel(slices, *refs):
    pieces = len(refs) - 8
    spots, parts = refs[0], refs[1 : 1 + pieces]
    weights, gain = refs[1 + pieces : 3 + pieces], refs[3 + pieces]
    outs, gain_out = refs[4 + pieces : 7 + pieces], refs[7 + pieces]
    width = outs[0].shape[1] // slices
    found = 0.0
    for k in range(pieces):
        for i in range(parts[k].shape[0]):
            spot = spots[k * parts[k].shape[0] + i]
            columns = pl.ds(pl.multiple_of(spot * width, width), width)
            for j in range(2):
                part = parts[k][i, :, j * width : (j + 1) * width].astype(F32)
                outs[j][:, columns] = part * gain[...]
                found = found + part * weights[j][:, columns].astype(F32)
            outs[2][:, columns] = parts[k][i, :, 2 * width :].astype(F32)
    gain_out[...] = jnp.sum(found, axis=1, keepdims=True)


def finish(parts, spots, weights, gain):
    rows = gain.shape[0]
    return in_vmem(
        functools.partial(finish_kernel, sum(part.shape[0] for part in parts)),
        list(parts) + list(weights) + [gain],
        [jax.ShapeDtypeStruct(weights[0].shape, F32)] * 3 + [jax.ShapeDtypeStruct((rows, 1), F32)],
        [],
        spots,
    )


def skipping(kernel, at, count):
    return lambda *refs: kernel(*refs[:at], *refs[at + count :])


def in_vmem(kernel, operands, outs, scratch, places=None, ties=()):
    first = [] if places is None else [places]
    kernel = skipping(kernel, len(first) + len(operands), len(ties))
    return pl.pallas_call(
        kernel,
        out_shape=outs,
        in_specs=[pl.BlockSpec(memory_space=pltpu.SMEM)] * len(first)
        + kernel_specs(len(operands))
        + [pl.BlockSpec(memory_space=pl.ANY)] * len(ties),
        out_specs=kernel_specs(len(outs)),
        scratch_shapes=scratch,
        compiler_params=pltpu.CompilerParams(vmem_limit_bytes=VMEM_BYTES),
        cost_estimate=pl.CostEstimate(flops=1, bytes_accessed=1, transcendentals=0),
    )(*first, *operands, *ties)


def kernel_specs(count):
    return [pl.BlockSpec(memory_space=pltpu.VMEM)] * count


def attention_forward(seq, q_cols, kv_cols, ties):
    length = seq.shape[0]
    return in_vmem(
        functools.partial(forward_kernel, q_cols, kv_cols),
        [seq],
        [
            jax.ShapeDtypeStruct((length, q_cols), BF),
            jax.ShapeDtypeStruct((q_cols // HEAD_DIM, length), F32),
        ],
        [],
        ties=ties,
    )


def attention_backward(seq, grads, logsums, q_cols, kv_cols):
    length = seq.shape[0]
    return in_vmem(
        functools.partial(backward_kernel, q_cols, kv_cols),
        [seq, grads, logsums],
        [jax.ShapeDtypeStruct(seq.shape, BF)],
        [pltpu.VMEM((length, HEAD_DIM), F32)] * 2,
    )[0]


def body(
    inputs,
    positions,
    attn_gain,
    q_weight,
    k_weight,
    v_weight,
    o_weight,
    ffn_gain,
    gate_weight,
    up_weight,
    down_weight,
    cotangent,
):
    sizes = {axis: lax.axis_size(axis) for axis in "yczx"}
    yn, cn, zn, xn = [sizes[axis] for axis in "yczx"]
    _, span, width = inputs.shape
    slices = yn * xn
    expanded = max(KV_HEADS, 2 * slices)
    copies = expanded // KV_HEADS
    rows = q_weight.shape[0]
    halves = zn // yn
    q_cols = HEADS * HEAD_DIM // (slices * halves)
    kv_cols = expanded * HEAD_DIM // (slices * halves)
    part_cols = q_cols + 2 * kv_cols
    piece = xn * span
    length = zn * piece

    states = reorder(inputs.reshape(span, width), sizes, "yczx", F32)
    grad_low = reorder(cotangent.reshape(span, width), sizes, "yczx", BF)

    gain_one = attn_gain.astype(F32)[:, None]
    gain_two = ffn_gain.astype(F32)[:, None]

    def widen(weight):
        return jnp.repeat(weight.reshape(rows, KV_HEADS, HEAD_DIM), copies, axis=1)

    def parts(weight, cols):
        return weight.reshape(rows, slices, halves, cols)

    wide_k, wide_v = widen(k_weight), widen(v_weight)
    qkv_rows = (
        jnp.concatenate(
            [parts(q_weight, q_cols), parts(wide_k, kv_cols), parts(wide_v, kv_cols)], axis=3
        )
        .reshape(rows, slices, halves * part_cols)
        .transpose(1, 0, 2)
    )
    qkv_scaled = (qkv_rows.astype(F32) * gain_one[None]).astype(BF)
    gate_scaled = (gate_weight.astype(F32) * gain_two).astype(BF)
    up_scaled = (up_weight.astype(F32) * gain_two).astype(BF)

    unit_one, factor_one = norm_of(states)
    o_rows = o_weight.reshape(rows, slices, halves * q_cols).transpose(1, 0, 2)
    near_attn = in_order(swap(jnp.concatenate([qkv_scaled, o_rows], axis=2), PLANE), PLANE)
    ffn_near = ffn_weights_near((gate_scaled, up_scaled, down_weight), sizes)
    digits = jnp.stack([positions.reshape(span) // 128, positions.reshape(span) % 128], axis=1)
    digits = jnp.repeat(digits.astype(BF), HEAD_DIM, axis=1)
    tokens_one = lax.all_gather(
        jnp.concatenate([unit_one.astype(BF), digits], axis=1), PLANE, axis=0, tiled=True
    )
    ffn_full = ffn_weights_far(after(ffn_near, near_attn))
    qkv_width = halves * part_cols
    qkv_own = spread(after(near_attn[..., :qkv_width], ffn_near), "z")
    o_own = spread(after(near_attn[..., qkv_width:], *qkv_own[1:]), "z")
    qkv_full = attention_weights(qkv_own, sizes)
    digits = tokens_one[:, width:].astype(F32)
    cosine, sine = angles_of(digits[:, 0] * 128.0 + digits[:, HEAD_DIM])
    cosine = jnp.concatenate([cosine] * 4, axis=1)
    sine = jnp.concatenate([-sine, sine] * 2, axis=1)
    rotated = ([True] * ((q_cols + kv_cols) // HEAD_DIM) + [False] * (kv_cols // HEAD_DIM)) * halves
    count = slices * span

    (packed,) = in_vmem(
        functools.partial(qkv_kernel, halves, rotated),
        [tokens_one, qkv_full, cosine, sine],
        [jax.ShapeDtypeStruct((zn, piece, part_cols), BF)],
        [],
    )
    heads_in = all_to_all(packed, "z").reshape(length, part_cols)
    attended, logsums = attention_forward(heads_in, q_cols, kv_cols, o_own[1:])
    o_full = attention_weights(o_own, sizes)
    grad_near = lax.all_gather(after(grad_low, attended), "z", axis=0, tiled=False)
    attended = all_to_all(attended.reshape(zn, piece, q_cols), "z")

    attn_tokens, o_part = in_vmem(
        functools.partial(o_kernel, halves),
        [attended, o_full],
        [
            jax.ShapeDtypeStruct((count, halves * q_cols), BF),
            jax.ShapeDtypeStruct((slices, span, width), BF),
        ],
        [],
    )
    square = jax.ShapeDtypeStruct((span, width), F32)
    hidden_one, unit_two, factor_two, tokens_near = in_vmem(
        hidden_norm_kernel,
        [all_to_all(o_part, PLANE), states],
        [
            square,
            square,
            jax.ShapeDtypeStruct((span, 1), F32),
            jax.ShapeDtypeStruct((zn, span, width), BF),
        ],
        [],
        ties=[ffn_full],
    )

    grad_far = trade(grad_near, "c", 1)
    tokens_near = all_to_all(tokens_near, "z")
    tokens_far = trade(tokens_near, "c", 1)
    tokens_near, tokens_far, grad_near, grad_far = [
        array.reshape(-1, width) for array in (tokens_near, tokens_far, grad_near, grad_far)
    ]
    z_far, dgate_far, dup_far, dx_far = ffn(tokens_far, grad_far, ffn_full, BF)
    z_near, dgate_near, dup_near, dx_near = ffn(
        tokens_near, grad_near, ffn_full, F32, [dx_far]
    )
    blocks = (zn, span, width)
    grad_both = dx_near.reshape(blocks) + trade(dx_far.reshape(blocks), "c", 1).astype(F32)
    grad_both = grad_both.astype(BF)
    grad_there = all_to_all(grad_both, "z")
    ffn_part = outer(
        (tokens_near, tokens_far),
        (grad_near, grad_far),
        (dgate_near, dgate_far),
        (dup_near, dup_far),
        (z_near, z_far),
    )
    result_far = add_product(z_far, ffn_full)
    result_near = add_product(z_near, ffn_full, trade(result_far, "c", 1)).reshape(blocks)
    grad_one, branch_tokens = in_vmem(
        norm_back_kernel,
        [grad_there, grad_low, unit_two, factor_two],
        [square, jax.ShapeDtypeStruct((slices, span, width), BF)],
        [],
        ties=[result_near, ffn_part],
    )
    result_there = swap(result_near, "z")

    branch_tokens = all_to_all(branch_tokens, PLANE).reshape(-1, width)
    (grad_attn,) = in_vmem(
        functools.partial(heads_kernel, halves),
        [branch_tokens, o_full],
        [jax.ShapeDtypeStruct((zn, piece, q_cols), BF)],
        [],
        ties=result_there[1:3],
    )
    ffn_sum = ffn_grads(after(ffn_part, grad_attn), sizes)
    grad_heads = all_to_all(grad_attn, "z")
    grad_heads = grad_heads.reshape(length, q_cols)
    heads_out = attention_backward(heads_in, grad_heads, logsums, q_cols, kv_cols)
    back = all_to_all(heads_out.reshape(zn, piece, part_cols), "z")
    ffn_sum, _ = ffn_grads_near(ffn_sum)
    grad_qkv, hat_part = in_vmem(
        functools.partial(qkv_back_kernel, halves, rotated),
        [back, qkv_full, cosine, sine],
        [
            jax.ShapeDtypeStruct((count, halves * part_cols), BF),
            jax.ShapeDtypeStruct((slices, span, width), BF),
        ],
        [],
    )
    grad_hat_one = after(scatter_plane(hat_part), result_there[3])
    input_grad = grad_one + norm_backward(grad_hat_one, unit_one, factor_one)
    qkv_part = contract_rows(tokens_one[:, :width], grad_qkv)
    qkv_sum, qkv_there, qkv_near = attention_grads(qkv_part, sizes, [], [])
    attn_tokens = after(attn_tokens, qkv_near)
    output = (after(hidden_one, qkv_near) + total(result_there)).astype(BF)
    o_sum, _, _ = attention_grads(contract_rows(branch_tokens, attn_tokens), sizes, qkv_there, [])
    attn_gain_grad = jnp.sum(qkv_sum * qkv_rows.astype(F32), axis=(0, 2))
    qkv_grad = (qkv_sum * gain_one[None]).transpose(1, 0, 2)
    qkv_grad = qkv_grad.reshape(rows, slices, halves, part_cols)
    spots = ffn_slices(sizes)
    gate_grad, up_grad, down_grad, ffn_gain_grad = finish(
        ffn_sum, spots, (gate_weight, up_weight), gain_two
    )

    def narrow(part):
        part = part.reshape(rows, KV_HEADS, copies, HEAD_DIM).sum(axis=2)
        return part.reshape(rows, KV_HEADS * HEAD_DIM)

    q_grad = qkv_grad[..., :q_cols].reshape(rows, HEADS * HEAD_DIM)
    k_grad = narrow(qkv_grad[..., q_cols : q_cols + kv_cols])
    v_grad = narrow(qkv_grad[..., q_cols + kv_cols :])
    return (
        reorder(output, sizes, "yxcz", BF).reshape(1, span, width),
        reorder(input_grad, sizes, "yxcz", F32).reshape(1, span, width),
        attn_gain_grad,
        q_grad,
        k_grad,
        v_grad,
        o_sum.transpose(1, 0, 2).reshape(rows, HEADS * HEAD_DIM),
        ffn_gain_grad.reshape(rows),
        gate_grad,
        up_grad,
        down_grad,
    )


def solution(mesh):
    batch, seq = mesh.devices.shape
    cores, column = 2, 4
    parts = mesh.devices.reshape(batch // cores, cores, column, seq // column)
    tokens = P(("y", "c"), ("z", "x"), None)
    rows = P(("y", "c", "z", "x"), None)
    gain = P(("y", "c", "z", "x"))
    return jax.shard_map(
        body,
        mesh=Mesh(parts, ("y", "c", "z", "x")),
        in_specs=(
            tokens, P(("y", "c"), ("z", "x")), gain, rows, rows, rows, rows, gain, rows, rows, rows,
            tokens,
        ),
        out_specs=(tokens, tokens, gain, rows, rows, rows, rows, gain, rows, rows, rows),
        check_vma=False,
    )
```
